256 devices in a mesh: row: 32 (over y, x, core), col: 8 (over z).
Axes of the slice: x: 4, y: 4, z: 8, core: 2. Of those that a mesh axis runs over, the one named last changes fastest.
Arguments:
- sigma_anc: bfloat16 [40, 256, 10240], P('col', 'row'), as said below
- lower_off: bfloat16 [8192, 4096], P('row', 'col'), may hold values from -0.01171875 to 0.01171875
- inverse_diag: bfloat16 [4096, 4096], P('row', 'col'), as said below
- structure: int32 [32], replicated, may hold values from 0 to 39, as said below
Outputs:
- sigma_off: bfloat16 [8192, 4096], P('row', 'col')
- sigma_front: float32 [4096, 4096], P('row', 'col')
The draws below stay inside these ranges and needn't reach their ends.
Inputs may be any that keep to these rules, and one draw needn't show every extreme that they name: `structure`: strictly increasing ancestor block indices. `sigma_anc`: exactly symmetric when read as a 10240 x 10240 matrix. `inverse_diag`: zero above the diagonal.
All inputs are finite; a program needn't handle non-finite values.
Results may differ from the reference program's by a relative error of at most 0.005.
Values may be sent and summed in bfloat16 or wider, within the bound.
A program may use at most 64 MiB of HBM per device.

```python
import math
import jax
import jax.numpy as jnp
from jax import lax

FRONT = 4096
BLOCK = 256
POSITIONS = 32
ROWS = 8192
ANC_BLOCKS = 40
ANC = 10240


def draw_sigma_anc(key, part):
    key = jax.random.fold_in(key, 11)
    first_key, second_key = jax.random.split(key)
    noise = jax.random.normal(first_key, (ANC, ANC), jnp.float32)
    sym = (noise + noise.T) * (0.9 / math.sqrt(2.0 * ANC))
    diagonal = jnp.exp(jax.random.uniform(second_key, (ANC,), jnp.float32, math.log(0.5), math.log(2.0)))
    whole = (sym + jnp.diag(diagonal)) * 32.0
    return whole.reshape(ANC_BLOCKS, BLOCK, ANC).astype(jnp.bfloat16)


def draw_inverse_diag(key, part):
    key = jax.random.fold_in(key, 23)
    first_key, second_key = jax.random.split(key, 2)
    below = jax.random.normal(first_key, (FRONT, FRONT), jnp.float32)
    below = below * (0.8 / math.sqrt(FRONT))
    diagonal = jnp.exp(jax.random.uniform(second_key, (FRONT,), jnp.float32, math.log(0.6), math.log(1.6)))
    row_ids = lax.broadcasted_iota(jnp.int32, (FRONT, FRONT), 0)
    col_ids = lax.broadcasted_iota(jnp.int32, (FRONT, FRONT), 1)
    return jnp.where(row_ids > col_ids, below, jnp.where(row_ids == col_ids, diagonal[:, None], 0.0)).astype(jnp.bfloat16)


def draw_structure(key, part):
    key = jax.random.fold_in(key, 37)
    inner = jax.random.permutation(key, ANC_BLOCKS - 2)[:POSITIONS - 2] + 1
    first = jnp.zeros((1,), jnp.int32)
    final = jnp.full((1,), ANC_BLOCKS - 1, jnp.int32)
    return jnp.sort(jnp.concatenate([first, inner.astype(jnp.int32), final])).astype(jnp.int32)


def level_of(rng, dims, shards, smallest, high):
    level, own = 1.0, jax.random.fold_in(rng, 6)
    for axis_at, blocks in shards:
        draws = jnp.exp(jax.random.uniform(jax.random.fold_in(own, axis_at), (blocks,), jnp.float32, smallest / len(shards), high / len(shards)))
        level = level * jnp.repeat(draws, dims[axis_at] // blocks).reshape([-1 if axis == axis_at else 1 for axis in range(len(dims))])
    return level


def normal_values(stream_key, dims, scale, limit, shards=(), kind=jnp.bfloat16):
    level = level_of(stream_key, dims, shards, -0.22, 0.18) if shards else 1.0
    entries = jax.random.normal(stream_key, dims, jnp.float32) * scale * level
    return jnp.minimum(jnp.maximum(entries, -limit), limit).astype(kind)


def setup_inputs(seed: int = 0) -> dict:
    arg_keys = jax.random.split(jax.random.key(seed), 5)
    sigma_anc = draw_sigma_anc(jax.random.fold_in(arg_keys[4], 71), 0)
    lower_off = normal_values(arg_keys[1], (ROWS, FRONT), (32 * ROWS) ** -0.5, 0.01171875, ((0, 32), (1, 8)))
    inverse_diag = draw_inverse_diag(jax.random.fold_in(arg_keys[4], 71), 0)
    structure = draw_structure(jax.random.fold_in(arg_keys[4], 71), 0)
    return {"sigma_anc": sigma_anc, "lower_off": lower_off, "inverse_diag": inverse_diag, "structure": structure}


def reference(sigma_anc, lower_off, inverse_diag, structure):
    count_blocks, block, order = sigma_anc.shape
    grid = sigma_anc.reshape(count_blocks, block, count_blocks, block)
    chosen = jnp.take(jnp.take(grid, structure, axis=0), structure, axis=2)
    total = structure.shape[0] * block
    sigma_ii = chosen.reshape(total, total)
    upper = jnp.dot(lower_off, inverse_diag, preferred_element_type=jnp.float32).astype(jnp.bfloat16)
    sigma_off = (-jnp.dot(sigma_ii, upper, preferred_element_type=jnp.float32)).astype(jnp.bfloat16)
    inverse_wide = inverse_diag.astype(jnp.float32)
    first = jnp.dot(inverse_wide.T, inverse_wide, precision=lax.Precision.HIGHEST)
    second = jnp.dot(sigma_off.astype(jnp.float32).T, upper.astype(jnp.float32), precision=lax.Precision.HIGHEST)
    return sigma_off, first - second
```

```python
import functools

import jax
import jax.numpy as jnp
from jax import lax
from jax.experimental import pallas as pl
from jax.experimental.pallas import tpu as pltpu
from jax.sharding import PartitionSpec as P

MESH = pl.DeviceIdType.MESH
NX, NY, NC, NZ = 4, 4, 2, 8
ANY = pl.BlockSpec(memory_space=pl.ANY)
VM = pl.BlockSpec(memory_space=pltpu.VMEM)
SM = pl.BlockSpec(memory_space=pltpu.SMEM)
BF = jnp.bfloat16


def coords():
    r = lax.axis_index("row")
    return r // 8, (r // 2) % 4, r % 2, lax.axis_index("col")


def column_slice(y, z):
    return (y + z // 2) % 4


def dev(y, x, c, z):
    return ((y * NX + x) * NC + c, z)


def greet(peers):
    sem = pltpu.get_barrier_semaphore()
    for peer in peers:
        pl.semaphore_signal(sem, inc=1, device_id=peer, device_id_type=MESH)
    pl.semaphore_wait(sem, len(peers))


class Links:
    def __init__(self, ss, rs):
        self.ss, self.rs, self.at, self.out = ss, rs, 0, []

    def slot(self, count=1):
        first = self.at
        self.at += count
        return first

    def send(self, i, src, dst, to):
        cp = pltpu.make_async_remote_copy(
            src_ref=src, dst_ref=dst, send_sem=self.ss.at[i], recv_sem=self.rs.at[i],
            device_id=to, device_id_type=MESH)
        cp.start()
        self.out.append(cp)

    def recv(self, i, dst, frm):
        pltpu.make_async_remote_copy(
            src_ref=dst, dst_ref=dst, send_sem=self.ss.at[i], recv_sem=self.rs.at[i],
            device_id=frm, device_id_type=MESH).wait_recv()

    def drain(self):
        for cp in self.out:
            cp.wait_send()


def ring(links, n, me, nxt, prv, view, own=None):
    steps = n // 2
    base = links.slot(4 * steps)
    own = own or (lambda h: view(me, h))
    idx = lambda d, s, h: base + (d * steps + s) * 2 + h
    for s in range(steps):
        for pos in range(1 if s == steps - 1 else 2):
            for d, h in ((0, pos), (1, 1 - pos)):
                shard = lax.rem(me + (n - s if d == 0 else s), n)
                if s:
                    yield
                    links.recv(idx(d, s - 1, h), view(shard, h), prv if d == 0 else nxt)
                src = own(h) if s == 0 else view(shard, h)
                links.send(idx(d, s, h), src, view(shard, h), nxt if d == 0 else prv)
    yield
    for s, pos in ((steps - 2, 1), (steps - 1, 0)):
        for d, h in ((0, pos), (1, 1 - pos)):
            shard = lax.rem(me + (n - s - 1 if d == 0 else s + 1), n)
            links.recv(idx(d, s, h), view(shard, h), prv if d == 0 else nxt)


def run(*gens):
    live = list(gens)
    while live:
        for g in list(live):
            try:
                next(g)
            except StopIteration:
                live.remove(g)


def remote_call(body, name, cid, outs, ins, in_specs, out_specs, nsem, scratch=(), vmem=60 * 2**20):
    return pl.pallas_call(
        body, out_shape=outs, in_specs=in_specs, out_specs=out_specs,
        scratch_shapes=[pltpu.SemaphoreType.DMA((nsem,)), pltpu.SemaphoreType.DMA((nsem,)),
                        pltpu.SemaphoreType.DMA((4,)), *scratch],
        compiler_params=pltpu.CompilerParams(
            collective_id=cid, has_side_effects=True, vmem_limit_bytes=vmem),
        name=name)(*ins)


def k1_body(low, diag, dsh, ssel, strip, dcols, dshard, s1, ss, rs, ls):
    y, x, c, z = coords()
    g = x * 2 + c
    links = Links(ss, rs)
    znext, zprev = dev(y, x, c, (z + 1) % NZ), dev(y, x, c, (z + 7) % NZ)
    line = [((g + d) % 8) for d in range(1, 8)]
    ydev = [dev((y + d) % NY, x, c, z) for d in range(1, 4)]
    ysrc = [(y + 4 - d) % NY for d in range(1, 4)]
    greet([znext, zprev] + [dev(y, q // 2, q % 2, z) for q in line] + ydev)

    def lview(shard, h):
        return strip.at[pl.ds(h * 128, 128), pl.ds(pl.multiple_of(shard * 512, 512), 512)]

    dslot = lambda t: dshard.at[pl.ds(pl.multiple_of(t * 128, 128), 128)]
    local = [
        pltpu.make_async_copy(low, strip.at[:, pl.ds(pl.multiple_of(z * 512, 512), 512)], ls.at[0]),
        pltpu.make_async_copy(diag, dcols.at[y, x, c], ls.at[1]),
        pltpu.make_async_copy(ssel.at[g], s1.at[g], ls.at[2]),
        pltpu.make_async_copy(dsh.at[column_slice(y, z)], dslot(y), ls.at[3]),
    ]
    lgen = ring(links, NZ, z, znext, zprev, lview, lambda h: low.at[pl.ds(h * 128, 128)])

    def dgen():
        sib = dev(y, x, 1 - c, z)
        xdev = [dev(y, (x + d) % NX, c, z) for d in range(1, 4)]
        xsrc = [(x + 4 - d) % NX for d in range(1, 4)]
        a, b = pl.ds(0, 64), pl.ds(64, 64)
        base = links.slot(12)
        sibs = links.slot(8)
        for d in range(3):
            links.send(base + d, diag.at[a], dcols.at[y, x, c, a], xdev[d])
            links.send(base + 3 + d, diag.at[b], dcols.at[y, x, c, b], ydev[d])
        for cp in local:
            cp.start()
        first = links.slot(14)
        for d in range(7):
            q = line[d]
            links.send(first + d, ssel.at[q], s1.at[g], dev(y, q // 2, q % 2, z))
        for d in range(3):
            t = (y + d + 1) % NY
            links.send(first + 7 + d, dsh.at[column_slice(t, z)], dslot(y), ydev[d])
        yield
        local[1].wait()
        for d in range(3):
            links.recv(base + d, dcols.at[y, xsrc[d], c, a], xdev[d])
        for d in range(3):
            links.send(base + 6 + d, dcols.at[y, :, c, a], dcols.at[y, :, c, a], ydev[d])
        links.send(sibs, dcols.at[y, :, c, a], dcols.at[y, :, c, a], sib)
        for d in range(3):
            links.recv(base + 3 + d, dcols.at[ysrc[d], x, c, b], ydev[d])
        for d in range(3):
            links.send(base + 9 + d, dcols.at[:, x, c, b], dcols.at[:, x, c, b], xdev[d])
        links.send(sibs + 1, dcols.at[:, x, c, b], dcols.at[:, x, c, b], sib)
        yield
        yield
        yield
        for d in (0, 2, 1):
            piece = dcols.at[ysrc[d], :, c, a]
            links.recv(base + 6 + d, piece, ydev[d])
            links.send(sibs + 2 + d, piece, piece, sib)
            piece = dcols.at[:, xsrc[d], c, b]
            links.recv(base + 9 + d, piece, xdev[d])
            links.send(sibs + 5 + d, piece, piece, sib)
            yield
        for d in range(7):
            s = (g + 8 - d - 1) % 8
            links.recv(first + d, s1.at[s], dev(y, s // 2, s % 2, z))
        for d in range(3):
            links.recv(first + 7 + d, dslot(ysrc[d]), ydev[d])
        yield
        o = 1 - c
        links.recv(sibs, dcols.at[y, :, o, a], sib)
        links.recv(sibs + 1, dcols.at[:, x, o, b], sib)
        for d in range(3):
            links.recv(sibs + 2 + d, dcols.at[ysrc[d], :, o, a], sib)
            links.recv(sibs + 5 + d, dcols.at[:, xsrc[d], o, b], sib)

    run(lgen, dgen())
    for k in (0, 2, 3):
        local[k].wait()
    links.drain()


def k2_body(ush, sblk, ubuf, sfull, ss, rs, ls):
    y, x, c, z = coords()
    links = Links(ss, rs)
    znext, zprev = dev(y, x, c, (z + 1) % NZ), dev(y, x, c, (z + 7) % NZ)
    ydev = [dev((y + d) % NY, x, c, z) for d in range(1, 4)]
    ysrc = [(y + 4 - d) % NY for d in range(1, 4)]
    greet([znext, zprev] + ydev)
    rows = lambda t: pl.ds(pl.multiple_of(t * 256, 256), 256)
    own = pltpu.make_async_copy(ush.at[column_slice(y, z)], ubuf.at[z, rows(y)], ls.at[0])
    base = links.slot(3)
    for d in range(3):
        links.send(base + d, ush.at[column_slice(y + d + 1, z)], ubuf.at[z, rows(y)], ydev[d])
    own.start()
    keep = pltpu.make_async_copy(sblk, sfull.at[y], ls.at[1])
    sgen = ring(links, NY, y, ydev[0], ydev[2], lambda t, h: sfull.at[t, pl.ds(h * 160, 160)],
                lambda h: sblk.at[pl.ds(h * 160, 160)])
    next(sgen)
    keep.start()
    own.wait()
    for d in range(3):
        links.recv(base + d, ubuf.at[z, rows(ysrc[d])], ydev[d])
    ugen = ring(links, NZ, z, znext, zprev, lambda t, h: ubuf.at[t, pl.ds(h * 512, 512)])
    next(ugen)
    for _ in range(4):
        next(ugen)
    run(ugen, sgen)
    keep.wait()
    links.drain()


def k3_body(part, structure, dshard, rows, dbuf, ss, rs, ls, pbuf, abuf, xbuf, fin, zbuf, snd):
    y, x, c, z = coords()
    g = x * 2 + c
    links = Links(ss, rs)
    zdev = [dev(y, x, c, (z + d) % NZ) for d in range(8)]
    sib = dev(y, x, 1 - c, z)
    plane = [(t, q) for t in range(4) for q in range(8)][1:]
    peer = lambda t, q: (((y + t) % NY) * 8 + (g + q) % 8, z)
    greet(zdev[1:] + [peer(t, q) for t, q in plane])
    order = [1, 3, 2, 0]
    base = links.slot(4)
    for d in order:
        t = (x + d) % NX
        links.send(base + d, part.at[2 * t + 1 - c], pbuf.at[d], sib)
    dgen = ring(links, NZ, z, zdev[1], zdev[7], lambda t, h: dbuf.at[t, pl.ds(h * 256, 256)],
                lambda h: dshard.at[pl.ds(h * 256, 256)])
    keep = pltpu.make_async_copy(dshard, dbuf.at[z], ls.at[0])
    keep.start()
    next(dgen)
    xs = links.slot(4)
    for d in order:
        t = (x + d) % NX
        links.recv(base + d, pbuf.at[d], sib)

        @pl.loop(0, 10)
        def _(i):
            at = pl.ds(pl.multiple_of(i * 16, 16), 16)
            total = part[2 * t + c, at].astype(jnp.float32) + pbuf[d, at].astype(jnp.float32)
            abuf[d, at] = total.astype(BF)

        if d:
            links.send(xs + d, abuf.at[d], xbuf.at[d - 1], dev(y, t, c, z))
    for _ in range(8):
        next(dgen)
    for d in (1, 3, 2):
        links.recv(xs + d, xbuf.at[d - 1], dev(y, (x + 4 - d) % NX, c, z))

    @pl.loop(0, 10)
    def _(i):
        at = pl.ds(pl.multiple_of(i * 16, 16), 16)
        total = abuf[0, at].astype(jnp.float32)
        for d in range(3):
            total = total + xbuf[d, at].astype(jnp.float32)
        total = (-total).astype(BF)
        for t in range(8):
            fin[t, i // 2, pl.ds(pl.multiple_of((i % 2) * 16, 16), 16)] = total[:, t * 128:(t + 1) * 128]

    zs = links.slot(8)
    slab = lambda k: zbuf.at[pl.ds(k * 5, 5)]
    for d in (4, 3, 5, 2, 6, 1, 7):
        links.send(zs + d, fin.at[(z + d) % NZ], slab(z), zdev[d])
    mine = pltpu.make_async_copy(fin.at[z], slab(z), ls.at[1])
    mine.start()
    for _ in dgen:
        pass
    keep.wait()
    mine.wait()
    for d in (1, 7, 2, 6, 3, 5, 4):
        links.recv(zs + d, slab((z + 8 - d) % NZ), zdev[8 - d])
    ps = links.slot(32)
    for q in range(8):
        for t in range(4):
            snd[q, t] = zbuf[structure[8 * t + q]]
    spot = lambda yy, gg: rows.at[:, gg, :, pl.ds(pl.multiple_of(column_slice(yy, z) * 128, 128), 128)]
    for t, q in plane:
        links.send(ps + 8 * t + q, snd.at[(g + q) % 8], spot(y, g), peer(t, q))
    home = pltpu.make_async_copy(snd.at[g], spot(y, g), ls.at[2])
    home.start()
    home.wait()
    for t, q in plane:
        links.recv(ps + 8 * t + q, spot((y + 4 - t) % 4, (g + 8 - q) % 8), peer(4 - t, 8 - q))
    links.drain()


def k4_body(fp, got, ss, rs, ls):
    y, x, c, z = coords()
    r = y * 8 + x * 2 + c
    g = x * 2 + c
    from_y = (r % 4 + 4 - r // 8) % 4
    is_self = from_y == y
    sem = pltpu.get_barrier_semaphore()
    dest = lambda k: 4 * k + column_slice(y, k)
    srcs = lambda q: from_y * 8 + q
    for k in range(8):
        @pl.when(dest(k) != r)
        def _():
            pl.semaphore_signal(sem, inc=1, device_id=(dest(k), z), device_id_type=MESH)

        @pl.when(srcs(k) != r)
        def _():
            pl.semaphore_signal(sem, inc=1, device_id=(srcs(k), z), device_id_type=MESH)
    pl.semaphore_wait(sem, jnp.where(is_self, 14, 16))

    def copy(k):
        return pltpu.make_async_remote_copy(
            src_ref=fp.at[k], dst_ref=got.at[g], send_sem=ss.at[k], recv_sem=rs.at[g],
            device_id=(dest(k), z), device_id_type=MESH)

    def incoming(q):
        return pltpu.make_async_remote_copy(
            src_ref=got.at[q], dst_ref=got.at[q], send_sem=ss.at[q], recv_sem=rs.at[q],
            device_id=(srcs(q), z), device_id_type=MESH)

    for k in range(8):
        @pl.when(dest(k) != r)
        def _():
            copy(k).start()

    @pl.when(is_self)
    def _():
        cp = pltpu.make_async_copy(fp.at[r // 4], got.at[g], ls.at[0])
        cp.start()
        cp.wait()

    for q in range(8):
        @pl.when(srcs(q) != r)
        def _():
            incoming(q).wait_recv()
    for k in range(8):
        @pl.when(dest(k) != r)
        def _():
            copy(k).wait_send()


def per_device(sigma_anc, lower_off, inverse_diag, structure):
    sds = jax.ShapeDtypeStruct
    blocks = sigma_anc.reshape(5, 8, 40, 256)
    ssel = jnp.take(blocks, structure, axis=2).reshape(5, 8, 4, 8, 256)
    ssel = jnp.transpose(ssel, (3, 2, 0, 1, 4)).reshape(8, 160, 256)
    dsh = jnp.transpose(inverse_diag.reshape(128, 4, 128), (1, 0, 2))
    strip, dcols, dshard, s1 = remote_call(
        k1_body, "gather_inputs", 1,
        (sds((256, 4096), BF), sds((4, 4, 2, 128, 512), BF), sds((512, 128), BF), sds((8, 160, 256), BF)),
        (lower_off, inverse_diag, dsh, ssel), [ANY] * 4, [ANY] * 4, 52)
    dmat = dcols.reshape(4096, 512)
    upper = jnp.dot(strip, dmat, preferred_element_type=jnp.float32).astype(BF)
    ush = jnp.transpose(upper.reshape(256, 4, 128), (1, 0, 2))
    sblk = jnp.transpose(s1.reshape(2, 4, 4, 5, 8, 256), (0, 3, 1, 4, 2, 5)).reshape(320, 1024)
    ubuf, sfull = remote_call(
        k2_body, "gather_upper", 2,
        (sds((8, 1024, 128), BF), sds((4, 320, 1024), BF)),
        (ush, sblk), [ANY] * 2, [ANY] * 2, 27)
    umat = jnp.transpose(ubuf, (1, 0, 2)).reshape(1024, 1024)
    part = jnp.dot(sfull.reshape(1280, 1024), umat, preferred_element_type=jnp.float32).astype(BF)
    rows, dbuf = remote_call(
        k3_body, "reduce_and_place", 3,
        (sds((4, 8, 32, 512), BF), sds((8, 512, 128), BF)),
        (part.reshape(8, 160, 1024), structure, dshard), [VM, SM, ANY], [VM, ANY], 64,
        [pltpu.VMEM((4, 160, 1024), BF), pltpu.VMEM((4, 160, 1024), BF), pltpu.VMEM((3, 160, 1024), BF),
         pltpu.VMEM((8, 5, 32, 128), BF), pltpu.VMEM((40, 32, 128), BF), pltpu.VMEM((8, 4, 32, 128), BF)])
    srows = rows.reshape(1024, 512)
    y, x, c, z = coords()
    sigma_off = lax.dynamic_slice_in_dim(srows, y * 256, 256, axis=0)
    drows = lax.dynamic_index_in_dim(dcols.reshape(4, 8, 128, 512), x * 2 + c, axis=1, keepdims=False)
    left = jnp.concatenate([ubuf, dbuf], axis=1)
    right = jnp.concatenate([-srows, drows.reshape(512, 512)], axis=0)
    fp = lax.dot_general(left, right, (((1,), (0,)), ((), ())), preferred_element_type=jnp.float32).astype(BF)
    got = remote_call(k4_body, "reduce_front", 4, sds((8, 128, 512), BF), (fp,), [ANY], ANY, 8)
    return sigma_off, jnp.sum(got.astype(jnp.float32), axis=0)


def solution(mesh):
    in_specs = (P("col", "row", None), P("row", "col"), P("row", "col"), P())
    out_specs = (P("row", "col"), P("row", "col"))
    return jax.shard_map(
        per_device, mesh=mesh, in_specs=in_specs, out_specs=out_specs, check_vma=False
    )
```

```python
import functools

import jax
import jax.numpy as jnp
from jax import lax
from jax.experimental import pallas as pl
from jax.experimental.pallas import tpu as pltpu
from jax.sharding import PartitionSpec as P

MESH = pl.DeviceIdType.MESH
NX, NY, NC, NZ = 4, 4, 2, 8
ANY = pl.BlockSpec(memory_space=pl.ANY)
VM = pl.BlockSpec(memory_space=pltpu.VMEM)
SM = pl.BlockSpec(memory_space=pltpu.SMEM)
BF = jnp.bfloat16


def coords():
    r = lax.axis_index("row")
    return r // 8, (r // 2) % 4, r % 2, lax.axis_index("col")


def column_slice(y, z):
    return (y + z // 2) % 4


def dev(y, x, c, z):
    return ((y * NX + x) * NC + c, z)


def greet(peers):
    sem = pltpu.get_barrier_semaphore()
    for peer in peers:
        pl.semaphore_signal(sem, inc=1, device_id=peer, device_id_type=MESH)
    pl.semaphore_wait(sem, len(peers))


class Links:
    def __init__(self, ss, rs):
        self.ss, self.rs, self.at, self.out = ss, rs, 0, []

    def slot(self, count=1):
        first = self.at
        self.at += count
        return first

    def send(self, i, src, dst, to):
        cp = pltpu.make_async_remote_copy(
            src_ref=src, dst_ref=dst, send_sem=self.ss.at[i], recv_sem=self.rs.at[i],
            device_id=to, device_id_type=MESH)
        cp.start()
        self.out.append(cp)

    def recv(self, i, dst, frm):
        pltpu.make_async_remote_copy(
            src_ref=dst, dst_ref=dst, send_sem=self.ss.at[i], recv_sem=self.rs.at[i],
            device_id=frm, device_id_type=MESH).wait_recv()

    def drain(self):
        for cp in self.out:
            cp.wait_send()


def ring(links, n, me, nxt, prv, view, own=None):
    steps = n // 2
    base = links.slot(4 * steps)
    own = own or (lambda h: view(me, h))
    idx = lambda d, s, h: base + (d * steps + s) * 2 + h
    for s in range(steps):
        for pos in range(1 if s == steps - 1 else 2):
            for d, h in ((0, pos), (1, 1 - pos)):
                shard = lax.rem(me + (n - s if d == 0 else s), n)
                if s:
                    yield
                    links.recv(idx(d, s - 1, h), view(shard, h), prv if d == 0 else nxt)
                src = own(h) if s == 0 else view(shard, h)
                links.send(idx(d, s, h), src, view(shard, h), nxt if d == 0 else prv)
    yield
    for s, pos in ((steps - 2, 1), (steps - 1, 0)):
        for d, h in ((0, pos), (1, 1 - pos)):
            shard = lax.rem(me + (n - s - 1 if d == 0 else s + 1), n)
            links.recv(idx(d, s, h), view(shard, h), prv if d == 0 else nxt)
        if pos:
            yield


def pull(gen):
    try:
        next(gen)
        return True
    except StopIteration:
        return False


def run(*gens):
    live = list(gens)
    while live:
        for g in list(live):
            try:
                next(g)
            except StopIteration:
                live.remove(g)


def mega(low, diag, dsh, ssel, structure, sig, front, ss, rs, ls,
         strip, dcols, dshard, s1, sblk, sfull, acc, ush, ubuf, dbuf,
         part, pbuf, abuf, xbuf, fin, zbuf, snd, rows, fp, got):
    y, x, c, z = coords()
    g = x * 2 + c
    r = y * 8 + g
    links = Links(ss, rs)
    zdev = [dev(y, x, c, (z + d) % NZ) for d in range(8)]
    xdev = [dev(y, (x + d) % NX, c, z) for d in range(4)]
    ydev = [dev((y + d) % NY, x, c, z) for d in range(4)]
    ysrc = [(y + 4 - d) % NY for d in range(4)]
    sib = dev(y, x, 1 - c, z)
    plane = [(t, q) for t in range(4) for q in range(8)][1:]
    peer = lambda t, q: (((y + t) % NY) * 8 + (g + q) % 8, z)
    greet(zdev[1:] + [peer(t, q) for t, q in plane])

    a, b = pl.ds(0, 64), pl.ds(64, 64)
    dslot = lambda t: dshard.at[pl.ds(pl.multiple_of(t * 128, 128), 128)]
    local = [
        pltpu.make_async_copy(low, strip.at[z], ls.at[0]),
        pltpu.make_async_copy(diag, dcols.at[y, x, c], ls.at[1]),
        pltpu.make_async_copy(ssel.at[g], s1.at[g], ls.at[2]),
        pltpu.make_async_copy(dsh.at[column_slice(y, z)], dslot(y), ls.at[3]),
    ]
    lgen = ring(links, NZ, z, zdev[1], zdev[7], lambda t, h: strip.at[t, pl.ds(h * 128, 128)],
                lambda h: low.at[pl.ds(h * 128, 128)])
    pull(lgen)
    a1 = ring(links, NY, y, ydev[1], ydev[3], lambda t, h: dcols.at[t, x, c, pl.ds(h * 32, 32)],
              lambda h: diag.at[pl.ds(h * 32, 32)])
    b1 = ring(links, NX, x, xdev[1], xdev[3], lambda t, h: dcols.at[y, t, c, pl.ds(64 + h * 32, 32)],
              lambda h: diag.at[pl.ds(64 + h * 32, 32)])
    pull(a1)
    pull(b1)
    for cp in (local[1], local[0], local[2], local[3]):
        cp.start()
    run(a1, b1)
    local[1].wait()
    a2 = ring(links, NX, x, xdev[1], xdev[3], lambda t, h: dcols.at[pl.ds(2 * h, 2), t, c, a])
    b2 = ring(links, NY, y, ydev[1], ydev[3], lambda t, h: dcols.at[t, pl.ds(2 * h, 2), c, b])
    pull(a2)
    pull(b2)
    first = links.slot(10)
    for d in (3, 2, 4, 1, 5, 0, 6):
        q = (g + d + 1) % 8
        links.send(first + d, ssel.at[q], s1.at[g], dev(y, q // 2, q % 2, z))
    for d in range(3):
        links.send(first + 7 + d, dsh.at[column_slice(y + d + 1, z)], dslot(y), ydev[d + 1])
    sibs = links.slot(8)

    def share(k, d):
        t = (x + 4 - d) % NX
        links.send(sibs + k, dcols.at[:, t, c, a], dcols.at[:, t, c, a], sib)
        t = ysrc[d]
        links.send(sibs + k + 1, dcols.at[t, :, c, b], dcols.at[t, :, c, b], sib)

    share(0, 0)
    for _ in range(2):
        pull(lgen)
        pull(lgen)
        pull(a2)
        pull(b2)
    for _ in range(2):
        pull(lgen)
        pull(lgen)
    pull(a2)
    pull(b2)
    share(2, 1)
    share(4, 3)
    for _ in range(2):
        pull(lgen)
    pull(a2)
    pull(b2)
    share(6, 2)

    local[2].wait()
    for d in range(7):
        s = (g + 8 - d - 1) % 8
        links.recv(first + d, s1.at[s], dev(y, s // 2, s % 2, z))

    @pl.loop(0, 2)
    def _(h):
        parts = [s1[4 * h + q].astype(jnp.float32).reshape(4, 5, 8, 256) for q in range(4)]
        for kb in range(4):
            for blk in range(5):
                tile = jnp.concatenate([p[kb, blk] for p in parts], axis=0).astype(BF)
                at = pl.ds(pl.multiple_of(h * 160 + blk * 32, 32), 32)
                sblk[at, kb * 256:(kb + 1) * 256] = tile

    keep = pltpu.make_async_copy(sblk, sfull.at[y], ls.at[2])
    keep.start()
    sgen = ring(links, NY, y, ydev[1], ydev[3], lambda t, h: sfull.at[t, pl.ds(h * 160, 160)],
                lambda h: sblk.at[pl.ds(h * 160, 160)])
    pull(sgen)
    while pull(lgen):
        pass
    for k, d in ((0, 0), (2, 1), (4, 3), (6, 2)):
        t = (x + 4 - d) % NX
        links.recv(sibs + k, dcols.at[:, t, 1 - c, a], sib)
        t = ysrc[d]
        links.recv(sibs + k + 1, dcols.at[t, :, 1 - c, b], sib)
    local[0].wait()

    acc[...] = jnp.zeros_like(acc)

    @pl.loop(0, 8)
    def _(k):
        right = dcols[k // 2, pl.ds((k % 2) * 2, 2)].reshape(512, 512)
        acc[...] += jnp.dot(strip[k], right, preferred_element_type=jnp.float32)

    for j in range(4):
        ush[j] = acc[:, j * 128:(j + 1) * 128].astype(BF)

    kblock = lambda t: pl.ds(pl.multiple_of(t * 256, 256), 256)
    own = pltpu.make_async_copy(ush.at[column_slice(y, z)], ubuf.at[z, kblock(y)], ls.at[0])
    base = links.slot(3)
    for d in range(3):
        links.send(base + d, ush.at[column_slice(y + d + 1, z)], ubuf.at[z, kblock(y)], ydev[d + 1])
    own.start()
    own.wait()
    for d in range(3):
        links.recv(base + d, ubuf.at[z, kblock(ysrc[d + 1])], ydev[3 - d])
    ugen = ring(links, NZ, z, zdev[1], zdev[7], lambda t, h: ubuf.at[t, pl.ds(h * 512, 512)])
    pull(ugen)
    local[3].wait()
    for d in range(3):
        links.recv(first + 7 + d, dslot(ysrc[d + 1]), ydev[3 - d])

    pair, xs, zs = links.slot(5), links.slot(15), links.slot(8)
    slab = lambda k: zbuf.at[pl.ds(k * 5, 5)]
    zkeep = pltpu.make_async_copy(fin.at[z], slab(z), ls.at[1])

    def shards(k):
        return ((z,), *[((z + d) % NZ, (z + NZ - d) % NZ) for d in (1, 2, 3)], ((z + 4) % NZ,))[k]

    def multiply(k):
        ids = shards(k)
        n = 128 * len(ids)
        right = jnp.concatenate([ubuf[t] for t in ids], axis=1) if len(ids) == 2 else ubuf[ids[0]]

        @pl.loop(0, 4)
        def _(i):
            total = jnp.dot(sfull[i], right, preferred_element_type=jnp.float32).astype(BF)
            part[k, i, 0, :, :n] = total[:160]
            part[k, i, 1, :, :n] = total[160:]

        links.send(pair + k, part.at[k, :, 1 - c, :, pl.ds(0, n)], pbuf.at[k, :, :, pl.ds(0, n)], sib)

    def across(k):
        n = 128 * len(shards(k))
        links.recv(pair + k, pbuf.at[k, :, :, pl.ds(0, n)], sib)

        @pl.loop(0, 4)
        def _(i):
            @pl.loop(0, 5)
            def _(j):
                at = pl.ds(pl.multiple_of(j * 32, 32), 32)
                total = part[k, i, c, at, :n].astype(jnp.float32) + pbuf[k, i, at, :n].astype(jnp.float32)
                abuf[k, i, at, :n] = total.astype(BF)

        for d in (2, 1, 3):
            links.send(xs + 3 * k + d - 1, abuf.at[k, (x + d) % NX, :, pl.ds(0, n)],
                       xbuf.at[k, d - 1, :, pl.ds(0, n)], xdev[d])

    def onward(k):
        ids = shards(k)
        n = 128 * len(ids)
        for d in (1, 3, 2):
            links.recv(xs + 3 * k + d - 1, xbuf.at[k, d - 1, :, pl.ds(0, n)], xdev[4 - d])

        @pl.loop(0, 5)
        def _(j):
            at = pl.ds(pl.multiple_of(j * 32, 32), 32)
            total = abuf[k, x, at, :n].astype(jnp.float32)
            for d in range(3):
                total = total + xbuf[k, d, at, :n].astype(jnp.float32)
            total = (-total).astype(BF)
            for m, t in enumerate(ids):
                fin[t, j] = total[:, m * 128:(m + 1) * 128]

        if k == 0:
            zkeep.start()
        else:
            for d in sorted({k, NZ - k}):
                links.send(zs + d, fin.at[(z + d) % NZ], slab(z), zdev[d])

    pull(sgen)
    pull(sgen)
    for _ in range(4):
        pull(ugen)
    while pull(sgen):
        pass
    keep.wait()
    multiply(0)
    multiply(1)
    across(0)
    for _ in range(4):
        pull(ugen)
    multiply(2)
    across(1)
    onward(0)
    for _ in range(3):
        pull(ugen)
    multiply(3)
    across(2)
    onward(1)
    pull(ugen)
    multiply(4)
    across(3)
    onward(2)
    across(4)
    onward(3)
    onward(4)
    dgen = ring(links, NZ, z, zdev[1], zdev[7], lambda t, h: dbuf.at[t, pl.ds(h * 256, 256)],
                lambda h: dshard.at[pl.ds(h * 256, 256)])
    dkeep = pltpu.make_async_copy(dshard, dbuf.at[z], ls.at[0])
    dkeep.start()
    pull(dgen)
    for _ in range(4):
        pull(dgen)
    zkeep.wait()
    for d in (1, 7, 2, 6, 3, 5, 4):
        links.recv(zs + d, slab((z + 8 - d) % NZ), zdev[8 - d])

    ps = links.slot(32)
    for q in range(8):
        for t in range(4):
            snd[q, t] = zbuf[structure[8 * t + q]]
    spot = lambda yy, gg: rows.at[:, gg, :, pl.ds(pl.multiple_of(column_slice(yy, z) * 128, 128), 128)]
    for t, q in plane:
        links.send(ps + 8 * t + q, snd.at[(g + q) % 8], spot(y, g), peer(t, q))
    home = pltpu.make_async_copy(snd.at[g], spot(y, g), ls.at[3])
    home.start()
    while pull(dgen):
        pass
    home.wait()
    dkeep.wait()
    for t, q in plane:
        links.recv(ps + 8 * t + q, spot((y + 4 - t) % 4, (g + 8 - q) % 8), peer(4 - t, 8 - q))
    sig[...] = rows[y].reshape(256, 512)

    fs = links.slot(8)
    from_y = (r % 4 + 4 - y) % 4
    is_self = from_y == y
    dest = lambda k: 4 * k + column_slice(y, k)
    src = lambda q: from_y * 8 + q

    def outgoing(k):
        return pltpu.make_async_remote_copy(
            src_ref=fp.at[k], dst_ref=got.at[g], send_sem=ss.at[fs + k], recv_sem=rs.at[fs + g],
            device_id=(dest(k), z), device_id_type=MESH)

    def incoming(q):
        return pltpu.make_async_remote_copy(
            src_ref=got.at[q], dst_ref=got.at[q], send_sem=ss.at[fs + q], recv_sem=rs.at[fs + q],
            device_id=(src(q), z), device_id_type=MESH)

    drows = dcols[:, x, c].reshape(512, 512)
    srows = rows[...].reshape(1024, 512)
    over_rows = (((0,), (0,)), ((), ()))
    for k in range(8):
        fp[k] = (
            lax.dot_general(dbuf[k], drows, over_rows, preferred_element_type=jnp.float32)
            - lax.dot_general(ubuf[k], srows, over_rows, preferred_element_type=jnp.float32)
        ).astype(BF)

        @pl.when(dest(k) != r)
        def _():
            outgoing(k).start()

    @pl.when(is_self)
    def _():
        got[g] = fp[r // 4]

    front[...] = jnp.zeros_like(front)
    for q in range(8):
        @pl.when(src(q) != r)
        def _():
            incoming(q).wait_recv()

        front[...] += got[q].astype(jnp.float32)
    for k in range(8):
        @pl.when(dest(k) != r)
        def _():
            outgoing(k).wait_send()
    links.drain()


def per_device(sigma_anc, lower_off, inverse_diag, structure):
    blocks = sigma_anc.reshape(5, 8, 40, 256)
    ssel = jnp.take(blocks, structure, axis=2).reshape(5, 8, 4, 8, 256)
    ssel = jnp.transpose(ssel, (3, 2, 0, 1, 4)).reshape(8, 160, 256)
    dsh = jnp.transpose(inverse_diag.reshape(128, 4, 128), (1, 0, 2))
    nsem = 210
    return pl.pallas_call(
        mega,
        out_shape=(jax.ShapeDtypeStruct((256, 512), BF), jax.ShapeDtypeStruct((128, 512), jnp.float32)),
        in_specs=[ANY] * 4 + [SM], out_specs=[VM, VM],
        scratch_shapes=[
            pltpu.SemaphoreType.DMA((nsem,)), pltpu.SemaphoreType.DMA((nsem,)), pltpu.SemaphoreType.DMA((4,)),
            pltpu.VMEM((8, 256, 512), BF), pltpu.VMEM((4, 4, 2, 128, 512), BF), pltpu.VMEM((512, 128), BF),
            pltpu.VMEM((8, 160, 256), BF), pltpu.VMEM((320, 1024), BF), pltpu.VMEM((4, 320, 1024), BF),
            pltpu.VMEM((256, 512), jnp.float32), pltpu.VMEM((4, 256, 128), BF), pltpu.VMEM((8, 1024, 128), BF),
            pltpu.VMEM((8, 512, 128), BF),
            pltpu.VMEM((5, 4, 2, 160, 256), BF), pltpu.VMEM((5, 4, 160, 256), BF),
            pltpu.VMEM((5, 4, 160, 256), BF), pltpu.VMEM((5, 3, 160, 256), BF),
            pltpu.VMEM((8, 5, 32, 128), BF), pltpu.VMEM((40, 32, 128), BF), pltpu.VMEM((8, 4, 32, 128), BF),
            pltpu.VMEM((4, 8, 32, 512), BF), pltpu.VMEM((8, 128, 512), BF), pltpu.VMEM((8, 128, 512), BF)],
        compiler_params=pltpu.CompilerParams(
            collective_id=1, has_side_effects=True, vmem_limit_bytes=60 * 2**20),
        name="selected_inverse")(lower_off, inverse_diag, dsh, ssel, structure)


def solution(mesh):
    in_specs = (P("col", "row", None), P("row", "col"), P("row", "col"), P())
    out_specs = (P("row", "col"), P("row", "col"))
    return jax.shard_map(
        per_device, mesh=mesh, in_specs=in_specs, out_specs=out_specs, check_vma=False
    )
```

```python
import functools

import jax
import jax.numpy as jnp
from jax import lax
from jax.experimental import pallas as pl
from jax.experimental.pallas import tpu as pltpu
from jax.sharding import PartitionSpec as P

MESH = pl.DeviceIdType.MESH
NX, NY, NC, NZ = 4, 4, 2, 8
ANY = pl.BlockSpec(memory_space=pl.ANY)
VM = pl.BlockSpec(memory_space=pltpu.VMEM)
SM = pl.BlockSpec(memory_space=pltpu.SMEM)
BF = jnp.bfloat16


def coords():
    r = lax.axis_index("row")
    return r // 8, (r // 2) % 4, r % 2, lax.axis_index("col")


def column_slice(y, z):
    return (y + z // 2) % 4


def dev(y, x, c, z):
    return ((y * NX + x) * NC + c, z)


def greet(peers):
    sem = pltpu.get_barrier_semaphore()
    for peer in peers:
        pl.semaphore_signal(sem, inc=1, device_id=peer, device_id_type=MESH)
    pl.semaphore_wait(sem, len(peers))


class Links:
    def __init__(self, ss, rs):
        self.ss, self.rs, self.at, self.out = ss, rs, 0, []

    def slot(self, count=1):
        first = self.at
        self.at += count
        return first

    def send(self, i, src, dst, to):
        cp = pltpu.make_async_remote_copy(
            src_ref=src, dst_ref=dst, send_sem=self.ss.at[i], recv_sem=self.rs.at[i],
            device_id=to, device_id_type=MESH)
        cp.start()
        self.out.append(cp)

    def recv(self, i, dst, frm):
        pltpu.make_async_remote_copy(
            src_ref=dst, dst_ref=dst, send_sem=self.ss.at[i], recv_sem=self.rs.at[i],
            device_id=frm, device_id_type=MESH).wait_recv()

    def drain(self):
        for cp in self.out:
            cp.wait_send()


def ring(links, n, me, nxt, prv, view, own=None, pause=False):
    steps = n // 2
    base = links.slot(4 * steps)
    own = own or (lambda h: view(me, h))
    idx = lambda d, s, h: base + (d * steps + s) * 2 + h
    for s in range(steps):
        for pos in range(1 if s == steps - 1 else 2):
            if pause and s == 0 and pos == 1:
                yield
            for d, h in ((0, pos), (1, 1 - pos)):
                shard = lax.rem(me + (n - s if d == 0 else s), n)
                if s:
                    yield
                    links.recv(idx(d, s - 1, h), view(shard, h), prv if d == 0 else nxt)
                src = own(h) if s == 0 else view(shard, h)
                links.send(idx(d, s, h), src, view(shard, h), nxt if d == 0 else prv)
    yield
    for s, pos in ((steps - 2, 1), (steps - 1, 0)):
        for d, h in ((0, pos), (1, 1 - pos)):
            shard = lax.rem(me + (n - s - 1 if d == 0 else s + 1), n)
            links.recv(idx(d, s, h), view(shard, h), prv if d == 0 else nxt)
        if pos:
            yield


def pull(gen):
    try:
        next(gen)
        return True
    except StopIteration:
        return False


def run(*gens):
    live = list(gens)
    while live:
        for g in list(live):
            try:
                next(g)
            except StopIteration:
                live.remove(g)


def choose(anc, structure, ssel):
    for q in range(8):
        picked = []
        for t in range(4):
            at = pl.ds(pl.multiple_of(structure[8 * t + q] * 256, 256), 256)
            picked.append(anc[:, :, at].astype(jnp.float32).reshape(40, 256))
        ssel[q] = jnp.concatenate(picked, axis=0).astype(BF)


def mega(low, diag, ssel, structure, sig, front, ss, rs, ls,

         strip, dcols, dshard, s1, sblk, sfull, acc, ush, ubuf, dbuf,
         part, pbuf, abuf, xbuf, fin, zbuf, snd, rows, fp, got, fpd, utr):
    y, x, c, z = coords()
    g = x * 2 + c
    r = y * 8 + g
    links = Links(ss, rs)
    zdev = [dev(y, x, c, (z + d) % NZ) for d in range(8)]
    xdev = [dev(y, (x + d) % NX, c, z) for d in range(4)]
    ydev = [dev((y + d) % NY, x, c, z) for d in range(4)]
    ysrc = [(y + 4 - d) % NY for d in range(4)]
    sib = dev(y, x, 1 - c, z)
    plane = [(t, q) for t in range(4) for q in range(8)][1:]
    peer = lambda t, q: (((y + t) % NY) * 8 + (g + q) % 8, z)
    greet([zdev[1], zdev[7]] + [peer(0, q) for q in range(1, 8)] + ydev[1:])

    a, b = pl.ds(0, 64), pl.ds(64, 64)
    dslot = lambda t: dshard.at[pl.ds(pl.multiple_of(t * 128, 128), 128)]
    dsl = lambda t: diag.at[:, pl.ds(pl.multiple_of(column_slice(t, z) * 128, 128), 128)]
    local = [
        pltpu.make_async_copy(low, strip.at[z], ls.at[0]),
        pltpu.make_async_copy(diag, dcols.at[y, x, c], ls.at[1]),
        pltpu.make_async_copy(ssel.at[g], s1.at[g], ls.at[2]),
        pltpu.make_async_copy(dsl(y), dslot(y), ls.at[3]),
    ]
    lgen = ring(links, NZ, z, zdev[1], zdev[7], lambda t, h: strip.at[t, pl.ds(h * 128, 128)],
                lambda h: low.at[pl.ds(h * 128, 128)])
    pull(lgen)
    a1 = ring(links, NY, y, ydev[1], ydev[3], lambda t, h: dcols.at[t, x, c, pl.ds(h * 32, 32)],
              lambda h: diag.at[pl.ds(h * 32, 32)])
    b1 = ring(links, NX, x, xdev[1], xdev[3], lambda t, h: dcols.at[y, t, c, pl.ds(64 + h * 32, 32)],
              lambda h: diag.at[pl.ds(64 + h * 32, 32)])
    pull(a1)
    pull(b1)
    for cp in (local[1], local[0], local[3]):
        cp.start()
    local[2].start()
    run(a1, b1)
    local[1].wait()
    a2 = ring(links, NX, x, xdev[1], xdev[3], lambda t, h: dcols.at[pl.ds(2 * h, 2), t, c, a])
    b2 = ring(links, NY, y, ydev[1], ydev[3], lambda t, h: dcols.at[t, pl.ds(2 * h, 2), c, b])
    pull(a2)
    pull(b2)
    first = links.slot(10)
    for d in (3, 2, 4, 1, 5, 0, 6):
        q = (g + d + 1) % 8
        links.send(first + d, ssel.at[q], s1.at[g], dev(y, q // 2, q % 2, z))
    for d in range(3):
        links.send(first + 7 + d, dsl(y + d + 1), dslot(y), ydev[d + 1])
    sibs = links.slot(8)

    def share(k, d):
        t = (x + 4 - d) % NX
        links.send(sibs + k, dcols.at[:, t, c, a], dcols.at[:, t, c, a], sib)
        t = ysrc[d]
        links.send(sibs + k + 1, dcols.at[t, :, c, b], dcols.at[t, :, c, b], sib)

    share(0, 0)
    for _ in range(2):
        pull(lgen)
        pull(lgen)
        pull(a2)
        pull(b2)
    for _ in range(2):
        pull(lgen)
        pull(lgen)
    pull(a2)
    pull(b2)
    share(2, 1)
    share(4, 3)
    for _ in range(2):
        pull(lgen)
    pull(a2)
    pull(b2)
    share(6, 2)

    local[2].wait()
    for d in range(7):
        s = (g + 8 - d - 1) % 8
        links.recv(first + d, s1.at[s], dev(y, s // 2, s % 2, z))

    @pl.loop(0, 2)
    def _(h):
        parts = [s1[4 * h + q].astype(jnp.float32).reshape(4, 5, 8, 256) for q in range(4)]
        for kb in range(4):
            for blk in range(5):
                tile = jnp.concatenate([p[kb, blk] for p in parts], axis=0).astype(BF)
                at = pl.ds(pl.multiple_of(h * 160 + blk * 32, 32), 32)
                sblk[at, kb * 256:(kb + 1) * 256] = tile

    keep = pltpu.make_async_copy(sblk, sfull.at[y], ls.at[2])
    keep.start()
    sgen = ring(links, NY, y, ydev[1], ydev[3], lambda t, h: sfull.at[t, pl.ds(h * 160, 160)],
                lambda h: sblk.at[pl.ds(h * 160, 160)], pause=True)
    pull(sgen)
    local[3].wait()
    for d in range(3):
        links.recv(first + 7 + d, dslot(ysrc[d + 1]), ydev[3 - d])
    dgen = ring(links, NZ, z, zdev[1], zdev[7], lambda t, h: dbuf.at[t, pl.ds(h * 256, 256)],
                lambda h: dshard.at[pl.ds(h * 256, 256)])
    dkeep = pltpu.make_async_copy(dshard, dbuf.at[z], ls.at[3])
    dkeep.start()
    pull(dgen)
    while pull(lgen):
        pass
    for k, d in ((0, 0), (2, 1), (4, 3), (6, 2)):
        t = (x + 4 - d) % NX
        links.recv(sibs + k, dcols.at[:, t, 1 - c, a], sib)
        t = ysrc[d]
        links.recv(sibs + k + 1, dcols.at[t, :, 1 - c, b], sib)
    local[0].wait()

    for _ in range(4):
        pull(dgen)
    acc[...] = jnp.zeros_like(acc)

    @pl.loop(0, 8)
    def _(k):
        right = dcols[k // 2, pl.ds((k % 2) * 2, 2)].reshape(512, 512)
        acc[...] += jnp.dot(strip[k], right, preferred_element_type=jnp.float32)

    for j in range(4):
        ush[j] = acc[:, j * 128:(j + 1) * 128].astype(BF)

    kblock = lambda t: pl.ds(pl.multiple_of(t * 256, 256), 256)
    own = pltpu.make_async_copy(ush.at[column_slice(y, z)], ubuf.at[z, kblock(y)], ls.at[0])
    base = links.slot(3)
    for d in range(3):
        links.send(base + d, ush.at[column_slice(y + d + 1, z)], ubuf.at[z, kblock(y)], ydev[d + 1])
    own.start()
    for _ in range(4):
        pull(dgen)
    pull(sgen)
    own.wait()
    for d in range(3):
        links.recv(base + d, ubuf.at[z, kblock(ysrc[d + 1])], ydev[3 - d])
    ugen = ring(links, NZ, z, zdev[1], zdev[7], lambda t, h: ubuf.at[t, pl.ds(h * 512, 512)])
    pull(ugen)
    for _ in range(2):
        pull(dgen)

    pair, xs, zs = links.slot(5), links.slot(15), links.slot(8)
    slab = lambda k: zbuf.at[pl.ds(k * 5, 5)]
    zkeep = pltpu.make_async_copy(fin.at[z], slab(z), ls.at[1])

    def shards(k):
        return ((z,), *[((z + d) % NZ, (z + NZ - d) % NZ) for d in (1, 2, 3)], ((z + 4) % NZ,))[k]

    def multiply(k):
        ids = shards(k)
        n = 128 * len(ids)
        right = jnp.concatenate([ubuf[t] for t in ids], axis=1) if len(ids) == 2 else ubuf[ids[0]]

        @pl.loop(0, 4)
        def _(i):
            total = jnp.dot(sfull[i], right, preferred_element_type=jnp.float32).astype(BF)
            part[k, i, 0, :, :n] = total[:160]
            part[k, i, 1, :, :n] = total[160:]

        links.send(pair + k, part.at[k, :, 1 - c, :, pl.ds(0, n)], pbuf.at[k, :, :, pl.ds(0, n)], sib)

    def across(k):
        n = 128 * len(shards(k))
        links.recv(pair + k, pbuf.at[k, :, :, pl.ds(0, n)], sib)

        @pl.loop(0, 4)
        def _(i):
            @pl.loop(0, 5)
            def _(j):
                at = pl.ds(pl.multiple_of(j * 32, 32), 32)
                total = part[k, i, c, at, :n].astype(jnp.float32) + pbuf[k, i, at, :n].astype(jnp.float32)
                abuf[k, i, at, :n] = total.astype(BF)

        for d in (2, 1, 3):
            links.send(xs + 3 * k + d - 1, abuf.at[k, (x + d) % NX, :, pl.ds(0, n)],
                       xbuf.at[k, d - 1, :, pl.ds(0, n)], xdev[d])

    def onward(k):
        ids = shards(k)
        n = 128 * len(ids)
        for d in (1, 3, 2):
            links.recv(xs + 3 * k + d - 1, xbuf.at[k, d - 1, :, pl.ds(0, n)], xdev[4 - d])

        @pl.loop(0, 5)
        def _(j):
            at = pl.ds(pl.multiple_of(j * 32, 32), 32)
            total = abuf[k, x, at, :n].astype(jnp.float32)
            for d in range(3):
                total = total + xbuf[k, d, at, :n].astype(jnp.float32)
            total = (-total).astype(BF)
            for m, t in enumerate(ids):
                fin[t, j] = total[:, m * 128:(m + 1) * 128]

        if k == 0:
            zkeep.start()
        else:
            for d in sorted({k, NZ - k}):
                links.send(zs + d, fin.at[(z + d) % NZ], slab(z), zdev[d])

    for _ in range(2):
        pull(sgen)
        pull(ugen)
        pull(ugen)
    for _ in range(2):
        pull(ugen)
        pull(ugen)
    while pull(sgen):
        pass
    keep.wait()
    multiply(0)
    multiply(1)
    across(0)
    multiply(2)
    across(1)
    onward(0)
    for _ in range(3):
        pull(ugen)
    multiply(3)
    across(2)
    onward(1)
    pull(ugen)
    multiply(4)
    across(3)
    onward(2)
    across(4)
    onward(3)
    onward(4)
    zkeep.wait()
    for d in (1, 7, 2, 6, 3, 5, 4):
        links.recv(zs + d, slab((z + 8 - d) % NZ), zdev[8 - d])

    ps = links.slot(32)
    for q in range(8):
        for t in range(4):
            snd[q, t] = zbuf[structure[8 * t + q]]
    spot = lambda yy, gg: rows.at[:, gg, :, pl.ds(pl.multiple_of(column_slice(yy, z) * 128, 128), 128)]
    for t, q in plane:
        links.send(ps + 8 * t + q, snd.at[(g + q) % 8], spot(y, g), peer(t, q))
    home = pltpu.make_async_copy(snd.at[g], spot(y, g), ls.at[0])
    home.start()
    while pull(dgen):
        pass
    dkeep.wait()
    over_rows = (((0,), (0,)), ((), ()))
    drows = dcols[:, x, c].reshape(512, 512)
    for k in range(8):
        fpd[k] = lax.dot_general(dbuf[k], drows, over_rows, preferred_element_type=jnp.float32)
        utr[k] = jnp.transpose(ubuf[k])
    home.wait()
    for t, q in plane:
        links.recv(ps + 8 * t + q, spot((y + 4 - t) % 4, (g + 8 - q) % 8), peer(4 - t, 8 - q))
    sig[...] = rows[y].reshape(256, 512)

    fs = links.slot(8)
    from_y = (r % 4 + 4 - y) % 4
    is_self = from_y == y
    dest = lambda k: 4 * k + column_slice(y, k)
    src = lambda q: from_y * 8 + q

    def outgoing(k):
        return pltpu.make_async_remote_copy(
            src_ref=fp.at[k], dst_ref=got.at[g], send_sem=ss.at[fs + k], recv_sem=rs.at[fs + g],
            device_id=(dest(k), z), device_id_type=MESH)

    def incoming(q):
        return pltpu.make_async_remote_copy(
            src_ref=got.at[q], dst_ref=got.at[q], send_sem=ss.at[fs + q], recv_sem=rs.at[fs + q],
            device_id=(src(q), z), device_id_type=MESH)

    srows = rows[...].reshape(1024, 512)
    for k in range(8):
        fp[k] = (fpd[k] - jnp.dot(utr[k], srows, preferred_element_type=jnp.float32)).astype(BF)

        @pl.when(dest(k) != r)
        def _():
            outgoing(k).start()

    @pl.when(is_self)
    def _():
        got[g] = fp[r // 4]

    front[...] = jnp.zeros_like(front)
    for q in range(8):
        @pl.when(src(q) != r)
        def _():
            incoming(q).wait_recv()

        front[...] += got[q].astype(jnp.float32)
    for k in range(8):
        @pl.when(dest(k) != r)
        def _():
            outgoing(k).wait_send()
    links.drain()


def per_device(sigma_anc, lower_off, inverse_diag, structure):
    ssel = pl.pallas_call(
        choose, out_shape=jax.ShapeDtypeStruct((8, 160, 256), BF), in_specs=[VM, SM], out_specs=VM,
        name="choose_columns")(sigma_anc, structure)
    nsem = 210
    return pl.pallas_call(
        mega,
        out_shape=(jax.ShapeDtypeStruct((256, 512), BF), jax.ShapeDtypeStruct((128, 512), jnp.float32)),
        in_specs=[ANY, ANY, ANY, SM], out_specs=[VM, VM],
        scratch_shapes=[
            pltpu.SemaphoreType.DMA((nsem,)), pltpu.SemaphoreType.DMA((nsem,)), pltpu.SemaphoreType.DMA((4,)),
            pltpu.VMEM((8, 256, 512), BF), pltpu.VMEM((4, 4, 2, 128, 512), BF), pltpu.VMEM((512, 128), BF),
            pltpu.VMEM((8, 160, 256), BF), pltpu.VMEM((320, 1024), BF), pltpu.VMEM((4, 320, 1024), BF),
            pltpu.VMEM((256, 512), jnp.float32), pltpu.VMEM((4, 256, 128), BF), pltpu.VMEM((8, 1024, 128), BF),
            pltpu.VMEM((8, 512, 128), BF),
            pltpu.VMEM((5, 4, 2, 160, 256), BF), pltpu.VMEM((5, 4, 160, 256), BF),
            pltpu.VMEM((5, 4, 160, 256), BF), pltpu.VMEM((5, 3, 160, 256), BF),
            pltpu.VMEM((8, 5, 32, 128), BF), pltpu.VMEM((40, 32, 128), BF), pltpu.VMEM((8, 4, 32, 128), BF),
            pltpu.VMEM((4, 8, 32, 512), BF), pltpu.VMEM((8, 128, 512), BF), pltpu.VMEM((8, 128, 512), BF),
            pltpu.VMEM((8, 128, 512), jnp.float32), pltpu.VMEM((8, 128, 1024), BF)],
        compiler_params=pltpu.CompilerParams(
            collective_id=1, has_side_effects=True, vmem_limit_bytes=60 * 2**20),
        name="selected_inverse")(lower_off, inverse_diag, ssel, structure)


def solution(mesh):
    in_specs = (P("col", "row", None), P("row", "col"), P("row", "col"), P())
    out_specs = (P("row", "col"), P("row", "col"))
    return jax.shard_map(
        per_device, mesh=mesh, in_specs=in_specs, out_specs=out_specs, check_vma=False
    )
```

```python
import functools

import jax
import jax.numpy as jnp
from jax import lax
from jax.experimental import pallas as pl
from jax.experimental.pallas import tpu as pltpu
from jax.sharding import PartitionSpec as P

MESH = pl.DeviceIdType.MESH
NX, NY, NC, NZ = 4, 4, 2, 8
ANY = pl.BlockSpec(memory_space=pl.ANY)
VM = pl.BlockSpec(memory_space=pltpu.VMEM)
SM = pl.BlockSpec(memory_space=pltpu.SMEM)
BF = jnp.bfloat16


def coords():
    r = lax.axis_index("row")
    return r // 8, (r // 2) % 4, r % 2, lax.axis_index("col")


def column_slice(y, z):
    return (y + z // 2) % 4


def dev(y, x, c, z):
    return ((y * NX + x) * NC + c, z)


def greet(peers):
    sem = pltpu.get_barrier_semaphore()
    for peer in peers:
        pl.semaphore_signal(sem, inc=1, device_id=peer, device_id_type=MESH)
    pl.semaphore_wait(sem, len(peers))


class Links:
    def __init__(self, ss, rs):
        self.ss, self.rs, self.at, self.out = ss, rs, 0, []

    def slot(self, count=1):
        first = self.at
        self.at += count
        return first

    def send(self, i, src, dst, to):
        cp = pltpu.make_async_remote_copy(
            src_ref=src, dst_ref=dst, send_sem=self.ss.at[i], recv_sem=self.rs.at[i],
            device_id=to, device_id_type=MESH)
        cp.start()
        self.out.append(cp)

    def recv(self, i, dst, frm):
        pltpu.make_async_remote_copy(
            src_ref=dst, dst_ref=dst, send_sem=self.ss.at[i], recv_sem=self.rs.at[i],
            device_id=frm, device_id_type=MESH).wait_recv()

    def drain(self):
        for cp in self.out:
            cp.wait_send()


def ring(links, n, me, nxt, prv, view, own=None, pieces=2, pause=False):
    steps, half = n // 2, pieces // 2
    base = links.slot(2 * pieces * steps)
    own = own or (lambda h: view(me, h))
    idx = lambda d, s, h: base + (d * steps + s) * pieces + h
    for s in range(steps):
        for pos in range(half if s == steps - 1 else pieces):
            if pause and s == 0 and pos == half:
                yield
            for d, h in ((0, pos), (1, pieces - 1 - pos)):
                shard = lax.rem(me + (n - s if d == 0 else s), n)
                if s:
                    yield
                    links.recv(idx(d, s - 1, h), view(shard, h), prv if d == 0 else nxt)
                src = own(h) if s == 0 else view(shard, h)
                links.send(idx(d, s, h), src, view(shard, h), nxt if d == 0 else prv)
    for s, first in ((steps - 2, half), (steps - 1, 0)):
        yield
        for pos in range(first, first + half):
            for d, h in ((0, pos), (1, pieces - 1 - pos)):
                shard = lax.rem(me + (n - s - 1 if d == 0 else s + 1), n)
                links.recv(idx(d, s, h), view(shard, h), prv if d == 0 else nxt)


def pull(gen):
    try:
        next(gen)
        return True
    except StopIteration:
        return False


def pulls(gen, count):
    for _ in range(count):
        pull(gen)


def run(*gens):
    live = list(gens)
    while live:
        for g in list(live):
            try:
                next(g)
            except StopIteration:
                live.remove(g)


def choose(anc, structure, ssel):
    for q in range(8):
        picked = []
        for t in range(4):
            at = pl.ds(pl.multiple_of(structure[8 * t + q] * 256, 256), 256)
            picked.append(anc[:, :, at].astype(jnp.float32).reshape(40, 256))
        ssel[q] = jnp.concatenate(picked, axis=0).astype(BF)


def mega(low, diag, ssel, structure, sig, front, ss, rs, ls,

         strip, dcols, dshard, s1, sblk, sfull, acc, ush, ubuf, dbuf,
         part, pbuf, abuf, xbuf, fin, zbuf, snd, rows, fp, fpair, fsum, got, fpd, utr):
    y, x, c, z = coords()
    g = x * 2 + c
    r = y * 8 + g
    links = Links(ss, rs)
    zdev = [dev(y, x, c, (z + d) % NZ) for d in range(8)]
    xdev = [dev(y, (x + d) % NX, c, z) for d in range(4)]
    ydev = [dev((y + d) % NY, x, c, z) for d in range(4)]
    ysrc = [(y + 4 - d) % NY for d in range(4)]
    sib = dev(y, x, 1 - c, z)
    plane = [(t, q) for t in range(4) for q in range(8)][1:]
    peer = lambda t, q: (((y + t) % NY) * 8 + (g + q) % 8, z)
    greet([zdev[1], zdev[7]] + [peer(0, q) for q in range(1, 8)] + ydev[1:])

    a, b = pl.ds(0, 96), pl.ds(96, 32)
    dslot = lambda t: dshard.at[pl.ds(pl.multiple_of(t * 128, 128), 128)]
    dsl = lambda t: diag.at[:, pl.ds(pl.multiple_of(column_slice(t, z) * 128, 128), 128)]
    local = [
        pltpu.make_async_copy(low, strip.at[z], ls.at[0]),
        pltpu.make_async_copy(diag, dcols.at[y, x, c], ls.at[1]),
        pltpu.make_async_copy(ssel.at[g], s1.at[g], ls.at[2]),
        pltpu.make_async_copy(dsl(y), dslot(y), ls.at[3]),
    ]
    lgen = ring(links, NZ, z, zdev[1], zdev[7], lambda t, h: strip.at[t, pl.ds(h * 64, 64)],
                lambda h: low.at[pl.ds(h * 64, 64)], 4)
    pull(lgen)
    a1 = ring(links, NY, y, ydev[1], ydev[3], lambda t, h: dcols.at[t, x, c, pl.ds(h * 48, 48)],
              lambda h: diag.at[pl.ds(h * 48, 48)])
    b1 = ring(links, NX, x, xdev[1], xdev[3], lambda t, h: dcols.at[y, t, c, pl.ds(96 + h * 16, 16)],
              lambda h: diag.at[pl.ds(96 + h * 16, 16)])
    pull(a1)
    pull(b1)
    first = links.slot(10)
    for d in (3, 2, 4, 1, 5, 0, 6):
        q = (g + d + 1) % 8
        links.send(first + d, ssel.at[q], s1.at[g], dev(y, q // 2, q % 2, z))
    for cp in (local[1], local[0], local[2], local[3]):
        cp.start()
    run(a1, b1)
    local[1].wait()
    a2 = ring(links, NX, x, xdev[1], xdev[3], lambda t, h: dcols.at[pl.ds(2 * h, 2), t, c, a])
    b2 = ring(links, NY, y, ydev[1], ydev[3], lambda t, h: dcols.at[t, pl.ds(2 * h, 2), c, b])
    pull(a2)
    pull(b2)
    for d in range(3):
        links.send(first + 7 + d, dsl(y + d + 1), dslot(y), ydev[d + 1])
    sibs = links.slot(8)

    def share(k, d):
        t = (x + 4 - d) % NX
        links.send(sibs + k, dcols.at[:, t, c, a], dcols.at[:, t, c, a], sib)
        t = ysrc[d]
        links.send(sibs + k + 1, dcols.at[t, :, c, b], dcols.at[t, :, c, b], sib)

    share(0, 0)
    pulls(lgen, 8)

    local[2].wait()
    for d in range(7):
        s = (g + 8 - d - 1) % 8
        links.recv(first + d, s1.at[s], dev(y, s // 2, s % 2, z))

    @pl.loop(0, 2)
    def _(h):
        parts = [s1[4 * h + q].astype(jnp.float32).reshape(4, 5, 8, 256) for q in range(4)]
        for kb in range(4):
            for blk in range(5):
                tile = jnp.concatenate([p[kb, blk] for p in parts], axis=0).astype(BF)
                at = pl.ds(pl.multiple_of(h * 160 + blk * 32, 32), 32)
                sblk[at, kb * 256:(kb + 1) * 256] = tile

    keep = pltpu.make_async_copy(sblk, sfull.at[y], ls.at[2])
    keep.start()
    sgen = ring(links, NY, y, ydev[1], ydev[3], lambda t, h: sfull.at[t, pl.ds(h * 160, 160)],
                lambda h: sblk.at[pl.ds(h * 160, 160)], pause=True)
    pull(sgen)
    for _ in range(2):
        pulls(lgen, 4)
        pull(a2)
        pull(b2)
    pull(a2)
    pull(b2)
    share(2, 1)
    share(4, 3)
    pulls(lgen, 4)
    pull(a2)
    pull(b2)
    share(6, 2)
    local[3].wait()
    for d in range(3):
        links.recv(first + 7 + d, dslot(ysrc[d + 1]), ydev[3 - d])
    dgen = ring(links, NZ, z, zdev[1], zdev[7], lambda t, h: dbuf.at[t, pl.ds(h * 256, 256)],
                lambda h: dshard.at[pl.ds(h * 256, 256)])
    dkeep = pltpu.make_async_copy(dshard, dbuf.at[z], ls.at[3])
    dkeep.start()
    pull(dgen)
    while pull(lgen):
        pass
    for k, d in ((0, 0), (2, 1), (4, 3), (6, 2)):
        t = (x + 4 - d) % NX
        links.recv(sibs + k, dcols.at[:, t, 1 - c, a], sib)
        t = ysrc[d]
        links.recv(sibs + k + 1, dcols.at[t, :, 1 - c, b], sib)
    local[0].wait()

    acc[...] = jnp.zeros_like(acc)

    @pl.loop(0, 8)
    def _(k):
        right = dcols[k // 2, pl.ds((k % 2) * 2, 2)].reshape(512, 512)
        acc[...] += jnp.dot(strip[k], right, preferred_element_type=jnp.float32)

    for j in range(4):
        ush[j] = acc[:, j * 128:(j + 1) * 128].astype(BF)

    kblock = lambda t: pl.ds(pl.multiple_of(t * 256, 256), 256)
    own = pltpu.make_async_copy(ush.at[column_slice(y, z)], ubuf.at[z, kblock(y)], ls.at[0])
    base = links.slot(3)
    for d in range(3):
        links.send(base + d, ush.at[column_slice(y + d + 1, z)], ubuf.at[z, kblock(y)], ydev[d + 1])
    own.start()
    pull(sgen)
    own.wait()
    for d in range(3):
        links.recv(base + d, ubuf.at[z, kblock(ysrc[d + 1])], ydev[3 - d])
    ugen = ring(links, NZ, z, zdev[1], zdev[7], lambda t, h: ubuf.at[t, pl.ds(h * 256, 256)], pieces=4)
    pull(ugen)
    pulls(sgen, 2)

    pair, xs, zs = links.slot(5), links.slot(15), links.slot(8)
    slab = lambda k: zbuf.at[pl.ds(k * 5, 5)]
    zkeep = pltpu.make_async_copy(fin.at[z], slab(z), ls.at[1])

    def shards(k):
        return ((z,), *[((z + d) % NZ, (z + NZ - d) % NZ) for d in (1, 2, 3)], ((z + 4) % NZ,))[k]

    def multiply(k):
        ids = shards(k)
        n = 128 * len(ids)
        right = jnp.concatenate([ubuf[t] for t in ids], axis=1) if len(ids) == 2 else ubuf[ids[0]]

        @pl.loop(0, 4)
        def _(i):
            total = jnp.dot(sfull[i], right, preferred_element_type=jnp.float32).astype(BF)
            part[k, i, 0, :, :n] = total[:160]
            part[k, i, 1, :, :n] = total[160:]

        links.send(pair + k, part.at[k, :, 1 - c, :, pl.ds(0, n)], pbuf.at[k, :, :, pl.ds(0, n)], sib)

    def across(k):
        n = 128 * len(shards(k))
        links.recv(pair + k, pbuf.at[k, :, :, pl.ds(0, n)], sib)

        @pl.loop(0, 4)
        def _(i):
            @pl.loop(0, 5)
            def _(j):
                at = pl.ds(pl.multiple_of(j * 32, 32), 32)
                total = part[k, i, c, at, :n].astype(jnp.float32) + pbuf[k, i, at, :n].astype(jnp.float32)
                abuf[k, i, at, :n] = total.astype(BF)

        for d in (2, 1, 3):
            links.send(xs + 3 * k + d - 1, abuf.at[k, (x + d) % NX, :, pl.ds(0, n)],
                       xbuf.at[k, d - 1, :, pl.ds(0, n)], xdev[d])

    def onward(k):
        ids = shards(k)
        n = 128 * len(ids)
        for d in (1, 3, 2):
            links.recv(xs + 3 * k + d - 1, xbuf.at[k, d - 1, :, pl.ds(0, n)], xdev[4 - d])

        @pl.loop(0, 5)
        def _(j):
            at = pl.ds(pl.multiple_of(j * 32, 32), 32)
            total = abuf[k, x, at, :n].astype(jnp.float32)
            for d in range(3):
                total = total + xbuf[k, d, at, :n].astype(jnp.float32)
            total = total.astype(BF)
            for m, t in enumerate(ids):
                fin[t, j] = total[:, m * 128:(m + 1) * 128]

        if k == 0:
            zkeep.start()
        else:
            for d in sorted({k, NZ - k}):
                links.send(zs + d, fin.at[(z + d) % NZ], slab(z), zdev[d])

    pulls(ugen, 8)
    while pull(sgen):
        pass
    keep.wait()
    multiply(0)
    multiply(1)
    across(0)
    pulls(ugen, 8)
    multiply(2)
    across(1)
    onward(0)
    pulls(ugen, 5)
    multiply(3)
    across(2)
    onward(1)
    pull(ugen)
    multiply(4)
    across(3)
    onward(2)
    across(4)
    onward(3)
    onward(4)
    zkeep.wait()
    for d in (1, 7, 2, 6, 3, 5, 4):
        links.recv(zs + d, slab((z + 8 - d) % NZ), zdev[8 - d])

    ps = links.slot(32)
    for q in range(8):
        for t in range(4):
            snd[q, t] = zbuf[structure[8 * t + q]]
    spot = lambda yy, gg: rows.at[:, gg, :, pl.ds(pl.multiple_of(column_slice(yy, z) * 128, 128), 128)]
    for t, q in plane:
        links.send(ps + 8 * t + q, snd.at[(g + q) % 8], spot(y, g), peer(t, q))
    home = pltpu.make_async_copy(snd.at[g], spot(y, g), ls.at[0])
    home.start()
    while pull(dgen):
        pass
    dkeep.wait()
    over_rows = (((0,), (0,)), ((), ()))
    drows = dcols[:, x, c].reshape(512, 512)
    for k in range(8):
        at = pl.ds((k % 2) * 128, 128)
        fpd[k // 2, at] = lax.dot_general(dbuf[k], drows, over_rows, preferred_element_type=jnp.float32)
        utr[k // 2, at] = jnp.transpose(ubuf[k])
    home.wait()
    for t, q in plane:
        links.recv(ps + 8 * t + q, spot((y + 4 - t) % 4, (g + 8 - q) % 8), peer(4 - t, 8 - q))
    sig[...] = rows[y].reshape(256, 512)

    srows = rows[...].reshape(1024, 512)
    cores, over_x = links.slot(2), links.slot(8)

    def product(k):
        return fpd[k] + jnp.dot(utr[k], srows, preferred_element_type=jnp.float32)

    for m in range(2):
        k = 2 * m + (y + 1 - c) % 2
        fp[m] = product(k).astype(BF)
        links.send(cores + m, fp.at[m], fpair.at[m], sib)

    def outgoing(m, e):
        k = 2 * m + (y + c) % 2
        j = (y + k) % 4
        to = (k * 8 + (2 * e + j // 2) * 2 + c, z)
        return to[0] != r, pltpu.make_async_remote_copy(
            src_ref=fsum.at[m, pl.ds(e * 128, 128)], dst_ref=got.at[x], send_sem=ss.at[over_x + 2 * m + e],
            recv_sem=rs.at[over_x + x], device_id=to, device_id_type=MESH)

    from_y = (r % 4 + 4 - y) % 4

    for m in range(2):
        k = 2 * m + (y + c) % 2
        total = product(k)
        links.recv(cores + m, fpair.at[m], sib)
        fsum[m] = (total + fpair[m].astype(jnp.float32)).astype(BF)
        for e in range(2):
            away, cp = outgoing(m, e)

            @pl.when(away)
            def _():
                cp.start()

            @pl.when(jnp.logical_not(away))
            def _():
                got[x] = fsum[m, e * 128:(e + 1) * 128]

    front[...] = jnp.zeros_like(front)
    for q in range(4):
        frm = from_y * 8 + q * 2 + c

        @pl.when(frm != r)
        def _():
            links.recv(over_x + q, got.at[q], (frm, z))

        front[...] += got[q].astype(jnp.float32)
    for m in range(2):
        for e in range(2):
            away, cp = outgoing(m, e)

            @pl.when(away)
            def _():
                cp.wait_send()
    links.drain()


def per_device(sigma_anc, lower_off, inverse_diag, structure):
    ssel = pl.pallas_call(
        choose, out_shape=jax.ShapeDtypeStruct((8, 160, 256), BF), in_specs=[VM, SM], out_specs=VM,
        name="choose_columns")(sigma_anc, structure)
    nsem = 256
    negated, front = pl.pallas_call(
        mega,
        out_shape=(jax.ShapeDtypeStruct((256, 512), BF), jax.ShapeDtypeStruct((128, 512), jnp.float32)),
        in_specs=[ANY, ANY, ANY, SM], out_specs=[VM, VM],
        scratch_shapes=[
            pltpu.SemaphoreType.DMA((nsem,)), pltpu.SemaphoreType.DMA((nsem,)), pltpu.SemaphoreType.DMA((4,)),
            pltpu.VMEM((8, 256, 512), BF), pltpu.VMEM((4, 4, 2, 128, 512), BF), pltpu.VMEM((512, 128), BF),
            pltpu.VMEM((8, 160, 256), BF), pltpu.VMEM((320, 1024), BF), pltpu.VMEM((4, 320, 1024), BF),
            pltpu.VMEM((256, 512), jnp.float32), pltpu.VMEM((4, 256, 128), BF), pltpu.VMEM((8, 1024, 128), BF),
            pltpu.VMEM((8, 512, 128), BF),
            pltpu.VMEM((5, 4, 2, 160, 256), BF), pltpu.VMEM((5, 4, 160, 256), BF),
            pltpu.VMEM((5, 4, 160, 256), BF), pltpu.VMEM((5, 3, 160, 256), BF),
            pltpu.VMEM((8, 5, 32, 128), BF), pltpu.VMEM((40, 32, 128), BF), pltpu.VMEM((8, 4, 32, 128), BF),
            pltpu.VMEM((4, 8, 32, 512), BF), pltpu.VMEM((2, 256, 512), BF), pltpu.VMEM((2, 256, 512), BF),
            pltpu.VMEM((2, 256, 512), BF), pltpu.VMEM((4, 128, 512), BF),
            pltpu.VMEM((4, 256, 512), jnp.float32), pltpu.VMEM((4, 256, 1024), BF)],
        compiler_params=pltpu.CompilerParams(
            collective_id=1, has_side_effects=True, vmem_limit_bytes=60 * 2**20),
        name="selected_inverse")(lower_off, inverse_diag, ssel, structure)
    return -negated, front


def solution(mesh):
    in_specs = (P("col", "row", None), P("row", "col"), P("row", "col"), P())
    out_specs = (P("row", "col"), P("row", "col"))
    return jax.shard_map(
        per_device, mesh=mesh, in_specs=in_specs, out_specs=out_specs, check_vma=False
    )
```

```python
import functools

import jax
import jax.numpy as jnp
from jax import lax
from jax.experimental import pallas as pl
from jax.experimental.pallas import tpu as pltpu
from jax.sharding import PartitionSpec as P

MESH = pl.DeviceIdType.MESH
NX, NY, NC, NZ = 4, 4, 2, 8
ANY = pl.BlockSpec(memory_space=pl.ANY)
VM = pl.BlockSpec(memory_space=pltpu.VMEM)
SM = pl.BlockSpec(memory_space=pltpu.SMEM)
BF = jnp.bfloat16


def coords():
    r = lax.axis_index("row")
    return r // 8, (r // 2) % 4, r % 2, lax.axis_index("col")


def column_slice(y, z):
    return (y + z // 2) % 4


def dev(y, x, c, z):
    return ((y * NX + x) * NC + c, z)


def greet(peers):
    sem = pltpu.get_barrier_semaphore()
    for peer in peers:
        pl.semaphore_signal(sem, inc=1, device_id=peer, device_id_type=MESH)
    pl.semaphore_wait(sem, len(peers))


class Links:
    def __init__(self, ss, rs):
        self.ss, self.rs, self.at, self.out = ss, rs, 0, []

    def slot(self, count=1):
        first = self.at
        self.at += count
        return first

    def send(self, i, src, dst, to):
        cp = pltpu.make_async_remote_copy(
            src_ref=src, dst_ref=dst, send_sem=self.ss.at[i], recv_sem=self.rs.at[i],
            device_id=to, device_id_type=MESH)
        cp.start()
        self.out.append(cp)

    def recv(self, i, dst, frm):
        pltpu.make_async_remote_copy(
            src_ref=dst, dst_ref=dst, send_sem=self.ss.at[i], recv_sem=self.rs.at[i],
            device_id=frm, device_id_type=MESH).wait_recv()

    def drain(self):
        for cp in self.out:
            cp.wait_send()


def ring(links, n, me, nxt, prv, view, own=None, pieces=2, pause=False):
    steps, half = n // 2, pieces // 2
    base = links.slot(2 * pieces * steps)
    own = own or (lambda h: view(me, h))
    idx = lambda d, s, h: base + (d * steps + s) * pieces + h
    for s in range(steps):
        for pos in range(half if s == steps - 1 else pieces):
            if pause and s == 0 and pos == half:
                yield
            for d, h in ((0, pos), (1, pieces - 1 - pos)):
                shard = lax.rem(me + (n - s if d == 0 else s), n)
                if s:
                    yield
                    links.recv(idx(d, s - 1, h), view(shard, h), prv if d == 0 else nxt)
                src = own(h) if s == 0 else view(shard, h)
                links.send(idx(d, s, h), src, view(shard, h), nxt if d == 0 else prv)
    for s, first in ((steps - 2, half), (steps - 1, 0)):
        yield
        for pos in range(first, first + half):
            for d, h in ((0, pos), (1, pieces - 1 - pos)):
                shard = lax.rem(me + (n - s - 1 if d == 0 else s + 1), n)
                links.recv(idx(d, s, h), view(shard, h), prv if d == 0 else nxt)


def pull(gen):
    try:
        next(gen)
        return True
    except StopIteration:
        return False


def pulls(gen, count):
    for _ in range(count):
        pull(gen)


def run(*gens):
    live = list(gens)
    while live:
        for g in list(live):
            try:
                next(g)
            except StopIteration:
                live.remove(g)


def choose(anc, structure, ssel):
    for q in range(8):
        picked = []
        for t in range(4):
            at = pl.ds(pl.multiple_of(structure[8 * t + q] * 256, 256), 256)
            picked.append(anc[:, :, at].astype(jnp.float32).reshape(40, 256))
        ssel[q] = jnp.concatenate(picked, axis=0).astype(BF)


def mega(low, diag, ssel, structure, sig, front, ss, rs, ls,

         strip, dcols, dshard, s1, sblk, sfull, acc, ush, ubuf, dbuf,
         part, pbuf, abuf, xbuf, fin, zbuf, snd, rows, fp, fpair, fsum, got, fpd, utr):
    y, x, c, z = coords()
    g = x * 2 + c
    r = y * 8 + g
    links = Links(ss, rs)
    zdev = [dev(y, x, c, (z + d) % NZ) for d in range(8)]
    xdev = [dev(y, (x + d) % NX, c, z) for d in range(4)]
    ydev = [dev((y + d) % NY, x, c, z) for d in range(4)]
    ysrc = [(y + 4 - d) % NY for d in range(4)]
    sib = dev(y, x, 1 - c, z)
    plane = [(t, q) for t in range(4) for q in range(8)][1:]
    peer = lambda t, q: (((y + t) % NY) * 8 + (g + q) % 8, z)
    greet([zdev[1], zdev[7]] + [peer(0, q) for q in range(1, 8)] + ydev[1:])

    a, b = pl.ds(0, 96), pl.ds(96, 32)
    dslot = lambda t: dshard.at[pl.ds(pl.multiple_of(t * 128, 128), 128)]
    dsl = lambda t: diag.at[:, pl.ds(pl.multiple_of(column_slice(t, z) * 128, 128), 128)]
    local = [
        pltpu.make_async_copy(low, strip.at[z], ls.at[0]),
        pltpu.make_async_copy(diag, dcols.at[y, x, c], ls.at[1]),
        pltpu.make_async_copy(ssel.at[g], s1.at[g], ls.at[2]),
        pltpu.make_async_copy(dsl(y), dslot(y), ls.at[3]),
    ]
    lgen = ring(links, NZ, z, zdev[1], zdev[7], lambda t, h: strip.at[t, pl.ds(h * 64, 64)],
                lambda h: low.at[pl.ds(h * 64, 64)], 4)
    pull(lgen)
    a1 = ring(links, NY, y, ydev[1], ydev[3], lambda t, h: dcols.at[t, x, c, pl.ds(h * 48, 48)],
              lambda h: diag.at[pl.ds(h * 48, 48)])
    b1 = ring(links, NX, x, xdev[1], xdev[3], lambda t, h: dcols.at[y, t, c, pl.ds(96 + h * 16, 16)],
              lambda h: diag.at[pl.ds(96 + h * 16, 16)])
    pull(a1)
    pull(b1)
    first = links.slot(10)
    for d in (3, 2, 4, 1, 5, 0, 6):
        q = (g + d + 1) % 8
        links.send(first + d, ssel.at[q], s1.at[g], dev(y, q // 2, q % 2, z))
    for cp in (local[1], local[0], local[2], local[3]):
        cp.start()
    run(a1, b1)
    local[1].wait()
    a2 = ring(links, NX, x, xdev[1], xdev[3], lambda t, h: dcols.at[pl.ds(2 * h, 2), t, c, a])
    b2 = ring(links, NY, y, ydev[1], ydev[3], lambda t, h: dcols.at[t, pl.ds(2 * h, 2), c, b])
    pull(a2)
    pull(b2)
    for d in range(3):
        links.send(first + 7 + d, dsl(y + d + 1), dslot(y), ydev[d + 1])
    sibs = links.slot(8)

    def share(k, d):
        t = (x + 4 - d) % NX
        links.send(sibs + k, dcols.at[:, t, c, a], dcols.at[:, t, c, a], sib)
        t = ysrc[d]
        links.send(sibs + k + 1, dcols.at[t, :, c, b], dcols.at[t, :, c, b], sib)

    share(0, 0)
    pulls(lgen, 8)

    local[2].wait()
    for d in range(7):
        s = (g + 8 - d - 1) % 8
        links.recv(first + d, s1.at[s], dev(y, s // 2, s % 2, z))

    @pl.loop(0, 2)
    def _(h):
        parts = [s1[4 * h + q].astype(jnp.float32).reshape(4, 5, 8, 256) for q in range(4)]
        for kb in range(4):
            for blk in range(5):
                tile = jnp.concatenate([p[kb, blk] for p in parts], axis=0).astype(BF)
                at = pl.ds(pl.multiple_of(h * 160 + blk * 32, 32), 32)
                sblk[at, kb * 256:(kb + 1) * 256] = tile

    keep = pltpu.make_async_copy(sblk, sfull.at[y], ls.at[2])
    keep.start()
    sgen = ring(links, NY, y, ydev[1], ydev[3], lambda t, h: sfull.at[t, pl.ds(h * 160, 160)],
                lambda h: sblk.at[pl.ds(h * 160, 160)], pause=True)
    pull(sgen)
    for _ in range(2):
        pulls(lgen, 4)
        pull(a2)
        pull(b2)
    pull(a2)
    pull(b2)
    share(2, 1)
    share(4, 3)
    pull(sgen)
    pulls(lgen, 4)
    pull(a2)
    pull(b2)
    share(6, 2)
    local[3].wait()
    for d in range(3):
        links.recv(first + 7 + d, dslot(ysrc[d + 1]), ydev[3 - d])
    dgen = ring(links, NZ, z, zdev[1], zdev[7], lambda t, h: dbuf.at[t, pl.ds(h * 256, 256)],
                lambda h: dshard.at[pl.ds(h * 256, 256)])
    dkeep = pltpu.make_async_copy(dshard, dbuf.at[z], ls.at[3])
    dkeep.start()
    pull(dgen)
    while pull(lgen):
        pass
    for k, d in ((0, 0), (2, 1), (4, 3), (6, 2)):
        t = (x + 4 - d) % NX
        links.recv(sibs + k, dcols.at[:, t, 1 - c, a], sib)
        t = ysrc[d]
        links.recv(sibs + k + 1, dcols.at[t, :, 1 - c, b], sib)
    local[0].wait()

    acc[...] = jnp.zeros_like(acc)

    @pl.loop(0, 8)
    def _(k):
        right = dcols[k // 2, pl.ds((k % 2) * 2, 2)].reshape(512, 512)
        acc[...] += jnp.dot(strip[k], right, preferred_element_type=jnp.float32)

    for j in range(4):
        ush[j] = acc[:, j * 128:(j + 1) * 128].astype(BF)

    kblock = lambda t: pl.ds(pl.multiple_of(t * 256, 256), 256)
    own = pltpu.make_async_copy(ush.at[column_slice(y, z)], ubuf.at[z, kblock(y)], ls.at[0])
    base = links.slot(3)
    for d in range(3):
        links.send(base + d, ush.at[column_slice(y + d + 1, z)], ubuf.at[z, kblock(y)], ydev[d + 1])
    own.start()
    own.wait()
    for d in range(3):
        links.recv(base + d, ubuf.at[z, kblock(ysrc[d + 1])], ydev[3 - d])
    ugen = ring(links, NZ, z, zdev[1], zdev[7], lambda t, h: ubuf.at[t, pl.ds(h * 256, 256)], pieces=4)
    pull(ugen)
    pulls(sgen, 2)

    pair, xs, zs = links.slot(5), links.slot(15), links.slot(8)
    slab = lambda k: zbuf.at[pl.ds(k * 5, 5)]
    zkeep = pltpu.make_async_copy(fin.at[z], slab(z), ls.at[1])

    def shards(k):
        return ((z,), *[((z + d) % NZ, (z + NZ - d) % NZ) for d in (1, 2, 3)], ((z + 4) % NZ,))[k]

    def multiply(k):
        ids = shards(k)
        n = 128 * len(ids)
        right = jnp.concatenate([ubuf[t] for t in ids], axis=1) if len(ids) == 2 else ubuf[ids[0]]

        @pl.loop(0, 4)
        def _(i):
            total = jnp.dot(sfull[i], right, preferred_element_type=jnp.float32).astype(BF)
            part[k, i, 0, :, :n] = total[:160]
            part[k, i, 1, :, :n] = total[160:]

        links.send(pair + k, part.at[k, :, 1 - c, :, pl.ds(0, n)], pbuf.at[k, :, :, pl.ds(0, n)], sib)

    def across(k):
        n = 128 * len(shards(k))
        links.recv(pair + k, pbuf.at[k, :, :, pl.ds(0, n)], sib)

        @pl.loop(0, 4)
        def _(i):
            @pl.loop(0, 5)
            def _(j):
                at = pl.ds(pl.multiple_of(j * 32, 32), 32)
                total = part[k, i, c, at, :n].astype(jnp.float32) + pbuf[k, i, at, :n].astype(jnp.float32)
                abuf[k, i, at, :n] = total.astype(BF)

        for d in (2, 1, 3):
            links.send(xs + 3 * k + d - 1, abuf.at[k, (x + d) % NX, :, pl.ds(0, n)],
                       xbuf.at[k, d - 1, :, pl.ds(0, n)], xdev[d])

    def onward(k):
        ids = shards(k)
        n = 128 * len(ids)
        for d in (1, 3, 2):
            links.recv(xs + 3 * k + d - 1, xbuf.at[k, d - 1, :, pl.ds(0, n)], xdev[4 - d])

        @pl.loop(0, 5)
        def _(j):
            at = pl.ds(pl.multiple_of(j * 32, 32), 32)
            total = abuf[k, x, at, :n].astype(jnp.float32)
            for d in range(3):
                total = total + xbuf[k, d, at, :n].astype(jnp.float32)
            total = total.astype(BF)
            for m, t in enumerate(ids):
                fin[t, j] = total[:, m * 128:(m + 1) * 128]

        if k == 0:
            zkeep.start()
        else:
            for d in sorted({k, NZ - k}):
                links.send(zs + d, fin.at[(z + d) % NZ], slab(z), zdev[d])

    pulls(ugen, 8)
    while pull(sgen):
        pass
    keep.wait()
    multiply(0)
    pulls(ugen, 4)
    multiply(1)
    across(0)
    pulls(ugen, 4)
    multiply(2)
    across(1)
    onward(0)
    pulls(ugen, 5)
    multiply(3)
    across(2)
    onward(1)
    pull(ugen)
    multiply(4)
    across(3)
    onward(2)
    across(4)
    onward(3)
    onward(4)
    zkeep.wait()
    for d in (1, 7, 2, 6, 3, 5, 4):
        links.recv(zs + d, slab((z + 8 - d) % NZ), zdev[8 - d])

    ps = links.slot(32)
    for q in range(8):
        for t in range(4):
            snd[q, t] = zbuf[structure[8 * t + q]]
    spot = lambda yy, gg: rows.at[column_slice(yy, z), :, gg]
    for t in (0, 1, 3, 2):
        for q in range(1 if t == 0 else 0, 8):
            links.send(ps + 8 * t + q, snd.at[(g + q) % 8], spot(y, g), peer(t, q))
    home = pltpu.make_async_copy(snd.at[g], spot(y, g), ls.at[0])
    home.start()
    while pull(dgen):
        pass
    dkeep.wait()
    over_rows = (((0,), (0,)), ((), ()))
    drows = dcols[:, x, c].reshape(512, 512)
    for k in range(8):
        at = pl.ds((k % 2) * 128, 128)
        both = lax.dot_general(dbuf[k], drows, over_rows, preferred_element_type=jnp.float32)
        for j in range(4):
            fpd[j, k // 2, at] = both[:, j * 128:(j + 1) * 128]
        utr[k // 2, at] = jnp.transpose(ubuf[k])
    home.wait()

    cores, over_x = links.slot(4), links.slot(16)
    from_y = (r % 4 + 4 - y) % 4
    theirs, ours = (y + 1 - c) % 2, (y + c) % 2

    def product(t, m, kind):
        k = 2 * m + kind
        slot = column_slice((y + 4 - t) % 4, z)
        right = rows[slot].reshape(1024, 128)
        return fpd[slot, k] + jnp.dot(utr[k], right, preferred_element_type=jnp.float32)

    def start_slice(t):
        for q in range(1 if t == 0 else 0, 8):
            links.recv(ps + 8 * t + q, spot((y + 4 - t) % 4, (g + 8 - q) % 8), peer(4 - t, 8 - q))
        for m in range(2):
            fp[t, m] = product(t, m, theirs).astype(BF)
        links.send(cores + t, fp.at[t], fpair.at[t], sib)

    def outgoing(t, m, e):
        k = 2 * m + ours
        to = (k * 8 + (2 * e + (y + k) % 4 // 2) * 2 + c, z)
        i = over_x + 4 * t
        return to[0] != r, pltpu.make_async_remote_copy(
            src_ref=fsum.at[t, m, pl.ds(e * 128, 128)], dst_ref=got.at[column_slice((y + 4 - t) % 4, z), x],
            send_sem=ss.at[i + 2 * m + e], recv_sem=rs.at[i + x], device_id=to, device_id_type=MESH)

    def finish_slice(t):
        for m in range(2):
            total = product(t, m, ours)
            if m == 0:
                links.recv(cores + t, fpair.at[t], sib)
            fsum[t, m] = (total + fpair[t, m].astype(jnp.float32)).astype(BF)
            for e in range(2):
                away, cp = outgoing(t, m, e)

                @pl.when(away)
                def _():
                    cp.start()

                @pl.when(jnp.logical_not(away))
                def _():
                    got[column_slice((y + 4 - t) % 4, z), x] = fsum[t, m, e * 128:(e + 1) * 128]

    turns = (0, 1, 3, 2)
    start_slice(turns[0])
    for before, t in zip(turns, turns[1:]):
        finish_slice(before)
        start_slice(t)
    finish_slice(turns[-1])
    for j in range(4):
        sig[:, j * 128:(j + 1) * 128] = rows[j, y].reshape(256, 128)

    for t in turns:
        slot = column_slice((from_y + 4 - t) % 4, z)
        for q in range(4):
            frm = from_y * 8 + q * 2 + c

            @pl.when(frm != r)
            def _():
                links.recv(over_x + 4 * t + q, got.at[slot, q], (frm, z))
    for j in range(4):
        total = got[j, 0].astype(jnp.float32)
        for q in range(1, 4):
            total = total + got[j, q].astype(jnp.float32)
        front[:, j * 128:(j + 1) * 128] = total
    for t in turns:
        for m in range(2):
            for e in range(2):
                away, cp = outgoing(t, m, e)

                @pl.when(away)
                def _():
                    cp.wait_send()
    links.drain()


def per_device(sigma_anc, lower_off, inverse_diag, structure):
    ssel = pl.pallas_call(
        choose, out_shape=jax.ShapeDtypeStruct((8, 160, 256), BF), in_specs=[VM, SM], out_specs=VM,
        name="choose_columns")(sigma_anc, structure)
    nsem = 272
    negated, front = pl.pallas_call(
        mega,
        out_shape=(jax.ShapeDtypeStruct((256, 512), BF), jax.ShapeDtypeStruct((128, 512), jnp.float32)),
        in_specs=[ANY, ANY, ANY, SM], out_specs=[VM, VM],
        scratch_shapes=[
            pltpu.SemaphoreType.DMA((nsem,)), pltpu.SemaphoreType.DMA((nsem,)), pltpu.SemaphoreType.DMA((4,)),
            pltpu.VMEM((8, 256, 512), BF), pltpu.VMEM((4, 4, 2, 128, 512), BF), pltpu.VMEM((512, 128), BF),
            pltpu.VMEM((8, 160, 256), BF), pltpu.VMEM((320, 1024), BF), pltpu.VMEM((4, 320, 1024), BF),
            pltpu.VMEM((256, 512), jnp.float32), pltpu.VMEM((4, 256, 128), BF), pltpu.VMEM((8, 1024, 128), BF),
            pltpu.VMEM((8, 512, 128), BF),
            pltpu.VMEM((5, 4, 2, 160, 256), BF), pltpu.VMEM((5, 4, 160, 256), BF),
            pltpu.VMEM((5, 4, 160, 256), BF), pltpu.VMEM((5, 3, 160, 256), BF),
            pltpu.VMEM((8, 5, 32, 128), BF), pltpu.VMEM((40, 32, 128), BF), pltpu.VMEM((8, 4, 32, 128), BF),
            pltpu.VMEM((4, 4, 8, 32, 128), BF), pltpu.VMEM((4, 2, 256, 128), BF), pltpu.VMEM((4, 2, 256, 128), BF),
            pltpu.VMEM((4, 2, 256, 128), BF), pltpu.VMEM((4, 4, 128, 128), BF),
            pltpu.VMEM((4, 4, 256, 128), jnp.float32), pltpu.VMEM((4, 256, 1024), BF)],
        compiler_params=pltpu.CompilerParams(
            collective_id=1, has_side_effects=True, vmem_limit_bytes=60 * 2**20),
        name="selected_inverse")(lower_off, inverse_diag, ssel, structure)
    return -negated, front


def solution(mesh):
    in_specs = (P("col", "row", None), P("row", "col"), P("row", "col"), P())
    out_specs = (P("row", "col"), P("row", "col"))
    return jax.shard_map(
        per_device, mesh=mesh, in_specs=in_specs, out_specs=out_specs, check_vma=False
    )
```

```python
import functools

import jax
import jax.numpy as jnp
from jax import lax
from jax.experimental import pallas as pl
from jax.experimental.pallas import tpu as pltpu
from jax.sharding import PartitionSpec as P

MESH = pl.DeviceIdType.MESH
NX, NY, NC, NZ = 4, 4, 2, 8
ANY = pl.BlockSpec(memory_space=pl.ANY)
VM = pl.BlockSpec(memory_space=pltpu.VMEM)
SM = pl.BlockSpec(memory_space=pltpu.SMEM)
BF = jnp.bfloat16


def coords():
    r = lax.axis_index("row")
    return r // 8, (r // 2) % 4, r % 2, lax.axis_index("col")


def column_slice(y, z):
    return (y + z // 2) % 4


def dev(y, x, c, z):
    return ((y * NX + x) * NC + c, z)


class Links:
    def __init__(self, ss, rs):
        self.ss, self.rs, self.at, self.out = ss, rs, 0, []

    def slot(self, count=1):
        first = self.at
        self.at += count
        return first

    def send(self, i, src, dst, to):
        cp = pltpu.make_async_remote_copy(
            src_ref=src, dst_ref=dst, send_sem=self.ss.at[i], recv_sem=self.rs.at[i],
            device_id=to, device_id_type=MESH)
        cp.start()
        self.out.append(cp)

    def recv(self, i, dst, frm):
        pltpu.make_async_remote_copy(
            src_ref=dst, dst_ref=dst, send_sem=self.ss.at[i], recv_sem=self.rs.at[i],
            device_id=frm, device_id_type=MESH).wait_recv()

    def drain(self):
        for cp in self.out:
            cp.wait_send()


def ring(links, n, me, nxt, prv, view, own=None, pieces=2, pause=False):
    steps, half = n // 2, pieces // 2
    base = links.slot(2 * pieces * steps)
    own = own or (lambda h: view(me, h))
    idx = lambda d, s, h: base + (d * steps + s) * pieces + h
    for s in range(steps):
        for pos in range(half if s == steps - 1 else pieces):
            if pause and s == 0 and pos == half:
                yield
            for d, h in ((0, pos), (1, pieces - 1 - pos)):
                shard = lax.rem(me + (n - s if d == 0 else s), n)
                if s:
                    yield
                    links.recv(idx(d, s - 1, h), view(shard, h), prv if d == 0 else nxt)
                src = own(h) if s == 0 else view(shard, h)
                links.send(idx(d, s, h), src, view(shard, h), nxt if d == 0 else prv)
    for s, first in ((steps - 2, half), (steps - 1, 0)):
        yield
        for pos in range(first, first + half):
            for d, h in ((0, pos), (1, pieces - 1 - pos)):
                shard = lax.rem(me + (n - s - 1 if d == 0 else s + 1), n)
                links.recv(idx(d, s, h), view(shard, h), prv if d == 0 else nxt)


def pull(gen):
    try:
        next(gen)
        return True
    except StopIteration:
        return False


def pulls(gen, count):
    for _ in range(count):
        pull(gen)


def run(*gens):
    live = list(gens)
    while live:
        for g in list(live):
            try:
                next(g)
            except StopIteration:
                live.remove(g)


def finish(negated, total, sig, front):
    sig[...] = -negated[...]
    front[...] = total[...]


def mega(low, diag, anc, structure, sig, front, ss, rs, ls, ancb, ssel,

         strip, dcols, dshard, s1, sblk, sfull, acc, ush, ubuf, dbuf,
         part, pbuf, abuf, xbuf, fin, zbuf, snd, rows, fp, fpair, fsum, got, fpd, utr):
    y, x, c, z = coords()
    g = x * 2 + c
    r = y * 8 + g
    links = Links(ss, rs)
    zdev = [dev(y, x, c, (z + d) % NZ) for d in range(8)]
    xdev = [dev(y, (x + d) % NX, c, z) for d in range(4)]
    ydev = [dev((y + d) % NY, x, c, z) for d in range(4)]
    ysrc = [(y + 4 - d) % NY for d in range(4)]
    sib = dev(y, x, 1 - c, z)
    plane = [(t, q) for t in range(4) for q in range(8)][1:]
    peer = lambda t, q: (((y + t) % NY) * 8 + (g + q) % 8, z)
    near_by = [zdev[1], zdev[7]] + [peer(0, q) for q in range(1, 8)] + ydev[1:]
    entry = pltpu.get_barrier_semaphore()
    for other in near_by:
        pl.semaphore_signal(entry, inc=1, device_id=other, device_id_type=MESH)
    for k in range(40):
        ancb[k] = anc[:, :, k * 256:(k + 1) * 256].astype(jnp.float32)
    for q in range(8):
        picked = [ancb[structure[8 * t + q]].reshape(40, 256) for t in range(4)]
        ssel[q] = jnp.concatenate(picked, axis=0).astype(BF)
    pl.semaphore_wait(entry, len(near_by))

    a, b = pl.ds(0, 96), pl.ds(96, 32)
    dslot = lambda t: dshard.at[pl.ds(pl.multiple_of(t * 128, 128), 128)]
    dsl = lambda t: diag.at[:, pl.ds(pl.multiple_of(column_slice(t, z) * 128, 128), 128)]
    local = [
        pltpu.make_async_copy(low, strip.at[z], ls.at[0]),
        pltpu.make_async_copy(diag, dcols.at[y, x, c], ls.at[1]),
        pltpu.make_async_copy(ssel.at[g], s1.at[g], ls.at[2]),
        pltpu.make_async_copy(dsl(y), dslot(y), ls.at[3]),
    ]
    lgen = ring(links, NZ, z, zdev[1], zdev[7], lambda t, h: strip.at[t, pl.ds(h * 64, 64)],
                lambda h: low.at[pl.ds(h * 64, 64)], 4)
    pull(lgen)
    a1 = ring(links, NY, y, ydev[1], ydev[3], lambda t, h: dcols.at[t, x, c, pl.ds(h * 48, 48)],
              lambda h: diag.at[pl.ds(h * 48, 48)])
    b1 = ring(links, NX, x, xdev[1], xdev[3], lambda t, h: dcols.at[y, t, c, pl.ds(96 + h * 16, 16)],
              lambda h: diag.at[pl.ds(96 + h * 16, 16)])
    pull(a1)
    pull(b1)
    first = links.slot(10)
    for d in (3, 2, 4, 1, 5, 0, 6):
        q = (g + d + 1) % 8
        links.send(first + d, ssel.at[q], s1.at[g], dev(y, q // 2, q % 2, z))
    for cp in (local[1], local[0], local[2], local[3]):
        cp.start()
    run(a1, b1)
    local[1].wait()
    a2 = ring(links, NX, x, xdev[1], xdev[3], lambda t, h: dcols.at[pl.ds(2 * h, 2), t, c, a])
    b2 = ring(links, NY, y, ydev[1], ydev[3], lambda t, h: dcols.at[t, pl.ds(2 * h, 2), c, b])
    pull(a2)
    pull(b2)
    for d in range(3):
        links.send(first + 7 + d, dsl(y + d + 1), dslot(y), ydev[d + 1])
    sibs = links.slot(8)

    def share(k, d):
        t = (x + 4 - d) % NX
        links.send(sibs + k, dcols.at[:, t, c, a], dcols.at[:, t, c, a], sib)
        t = ysrc[d]
        links.send(sibs + k + 1, dcols.at[t, :, c, b], dcols.at[t, :, c, b], sib)

    share(0, 0)
    pulls(lgen, 8)

    local[2].wait()
    for d in range(7):
        s = (g + 8 - d - 1) % 8
        links.recv(first + d, s1.at[s], dev(y, s // 2, s % 2, z))

    @pl.loop(0, 2)
    def _(h):
        parts = [s1[4 * h + q].astype(jnp.float32).reshape(4, 5, 8, 256) for q in range(4)]
        for kb in range(4):
            for blk in range(5):
                tile = jnp.concatenate([p[kb, blk] for p in parts], axis=0).astype(BF)
                at = pl.ds(pl.multiple_of(h * 160 + blk * 32, 32), 32)
                sblk[at, kb * 256:(kb + 1) * 256] = tile

    keep = pltpu.make_async_copy(sblk, sfull.at[y], ls.at[2])
    keep.start()
    sgen = ring(links, NY, y, ydev[1], ydev[3], lambda t, h: sfull.at[t, pl.ds(h * 160, 160)],
                lambda h: sblk.at[pl.ds(h * 160, 160)], pause=True)
    pull(sgen)
    for _ in range(2):
        pulls(lgen, 4)
        pull(a2)
        pull(b2)
    pull(a2)
    pull(b2)
    share(2, 1)
    share(4, 3)
    pull(sgen)
    pulls(lgen, 4)
    pull(a2)
    pull(b2)
    share(6, 2)
    local[3].wait()
    for d in range(3):
        links.recv(first + 7 + d, dslot(ysrc[d + 1]), ydev[3 - d])
    dgen = ring(links, NZ, z, zdev[1], zdev[7], lambda t, h: dbuf.at[t, pl.ds(h * 256, 256)],
                lambda h: dshard.at[pl.ds(h * 256, 256)])
    dkeep = pltpu.make_async_copy(dshard, dbuf.at[z], ls.at[3])
    dkeep.start()
    pull(dgen)
    while pull(lgen):
        pass
    for k, d in ((0, 0), (2, 1), (4, 3), (6, 2)):
        t = (x + 4 - d) % NX
        links.recv(sibs + k, dcols.at[:, t, 1 - c, a], sib)
        t = ysrc[d]
        links.recv(sibs + k + 1, dcols.at[t, :, 1 - c, b], sib)
    local[0].wait()

    acc[...] = jnp.zeros_like(acc)

    @pl.loop(0, 8)
    def _(k):
        right = dcols[k // 2, pl.ds((k % 2) * 2, 2)].reshape(512, 512)
        acc[...] += jnp.dot(strip[k], right, preferred_element_type=jnp.float32)

    for j in range(4):
        ush[j] = acc[:, j * 128:(j + 1) * 128].astype(BF)

    kblock = lambda t: pl.ds(pl.multiple_of(t * 256, 256), 256)
    own = pltpu.make_async_copy(ush.at[column_slice(y, z)], ubuf.at[z, kblock(y)], ls.at[0])
    base = links.slot(3)
    for d in range(3):
        links.send(base + d, ush.at[column_slice(y + d + 1, z)], ubuf.at[z, kblock(y)], ydev[d + 1])
    own.start()
    own.wait()
    for d in range(3):
        links.recv(base + d, ubuf.at[z, kblock(ysrc[d + 1])], ydev[3 - d])
    ugen = ring(links, NZ, z, zdev[1], zdev[7], lambda t, h: ubuf.at[t, pl.ds(h * 256, 256)], pieces=4)
    pull(ugen)
    pulls(sgen, 2)

    pair, xs, zs = links.slot(5), links.slot(15), links.slot(8)
    slab = lambda k: zbuf.at[pl.ds(k * 5, 5)]
    zkeep = pltpu.make_async_copy(fin.at[z], slab(z), ls.at[1])

    def shards(k):
        return ((z,), *[((z + d) % NZ, (z + NZ - d) % NZ) for d in (1, 2, 3)], ((z + 4) % NZ,))[k]

    def multiply(k):
        ids = shards(k)
        n = 128 * len(ids)
        right = jnp.concatenate([ubuf[t] for t in ids], axis=1) if len(ids) == 2 else ubuf[ids[0]]

        @pl.loop(0, 4)
        def _(i):
            total = jnp.dot(sfull[i], right, preferred_element_type=jnp.float32).astype(BF)
            part[k, i, 0, :, :n] = total[:160]
            part[k, i, 1, :, :n] = total[160:]

        links.send(pair + k, part.at[k, :, 1 - c, :, pl.ds(0, n)], pbuf.at[k, :, :, pl.ds(0, n)], sib)

    def across(k):
        n = 128 * len(shards(k))
        links.recv(pair + k, pbuf.at[k, :, :, pl.ds(0, n)], sib)

        @pl.loop(0, 4)
        def _(i):
            @pl.loop(0, 5)
            def _(j):
                at = pl.ds(pl.multiple_of(j * 32, 32), 32)
                total = part[k, i, c, at, :n].astype(jnp.float32) + pbuf[k, i, at, :n].astype(jnp.float32)
                abuf[k, i, at, :n] = total.astype(BF)

        for d in (2, 1, 3):
            links.send(xs + 3 * k + d - 1, abuf.at[k, (x + d) % NX, :, pl.ds(0, n)],
                       xbuf.at[k, d - 1, :, pl.ds(0, n)], xdev[d])

    def onward(k):
        ids = shards(k)
        n = 128 * len(ids)
        for d in (1, 3, 2):
            links.recv(xs + 3 * k + d - 1, xbuf.at[k, d - 1, :, pl.ds(0, n)], xdev[4 - d])

        @pl.loop(0, 5)
        def _(j):
            at = pl.ds(pl.multiple_of(j * 32, 32), 32)
            total = abuf[k, x, at, :n].astype(jnp.float32)
            for d in range(3):
                total = total + xbuf[k, d, at, :n].astype(jnp.float32)
            total = total.astype(BF)
            for m, t in enumerate(ids):
                fin[t, j] = total[:, m * 128:(m + 1) * 128]

        if k == 0:
            zkeep.start()
        else:
            for d in sorted({k, NZ - k}):
                links.send(zs + d, fin.at[(z + d) % NZ], slab(z), zdev[d])

    pulls(ugen, 8)
    while pull(sgen):
        pass
    keep.wait()
    multiply(0)
    pulls(ugen, 4)
    multiply(1)
    across(0)
    pulls(ugen, 4)
    multiply(2)
    across(1)
    onward(0)
    pulls(ugen, 5)
    multiply(3)
    across(2)
    onward(1)
    pull(ugen)
    multiply(4)
    across(3)
    onward(2)
    across(4)
    onward(3)
    onward(4)
    zkeep.wait()
    for d in (1, 7, 2, 6, 3, 5, 4):
        links.recv(zs + d, slab((z + 8 - d) % NZ), zdev[8 - d])

    ps = links.slot(32)
    for q in range(8):
        for t in range(4):
            snd[q, t] = zbuf[structure[8 * t + q]]
    spot = lambda yy, gg: rows.at[column_slice(yy, z), :, gg]
    for t in (0, 1, 3, 2):
        for q in range(1 if t == 0 else 0, 8):
            links.send(ps + 8 * t + q, snd.at[(g + q) % 8], spot(y, g), peer(t, q))
    home = pltpu.make_async_copy(snd.at[g], spot(y, g), ls.at[0])
    home.start()
    while pull(dgen):
        pass
    dkeep.wait()
    over_rows = (((0,), (0,)), ((), ()))
    drows = dcols[:, x, c].reshape(512, 512)
    for k in range(8):
        at = pl.ds((k % 2) * 128, 128)
        both = lax.dot_general(dbuf[k], drows, over_rows, preferred_element_type=jnp.float32)
        for j in range(4):
            fpd[j, k // 2, at] = both[:, j * 128:(j + 1) * 128]
        utr[k // 2, at] = jnp.transpose(ubuf[k])
    home.wait()

    cores, over_x = links.slot(4), links.slot(16)
    from_y = (r % 4 + 4 - y) % 4
    theirs, ours = (y + 1 - c) % 2, (y + c) % 2

    def product(t, m, kind):
        k = 2 * m + kind
        slot = column_slice((y + 4 - t) % 4, z)
        right = rows[slot].reshape(1024, 128)
        return fpd[slot, k] + jnp.dot(utr[k], right, preferred_element_type=jnp.float32)

    def start_slice(t):
        for q in range(1 if t == 0 else 0, 8):
            links.recv(ps + 8 * t + q, spot((y + 4 - t) % 4, (g + 8 - q) % 8), peer(4 - t, 8 - q))
        for m in range(2):
            fp[t, m] = product(t, m, theirs).astype(BF)
        links.send(cores + t, fp.at[t], fpair.at[t], sib)

    def outgoing(t, m, e):
        k = 2 * m + ours
        to = (k * 8 + (2 * e + (y + k) % 4 // 2) * 2 + c, z)
        i = over_x + 4 * t
        return to[0] != r, pltpu.make_async_remote_copy(
            src_ref=fsum.at[t, m, pl.ds(e * 128, 128)], dst_ref=got.at[column_slice((y + 4 - t) % 4, z), x],
            send_sem=ss.at[i + 2 * m + e], recv_sem=rs.at[i + x], device_id=to, device_id_type=MESH)

    def finish_slice(t):
        for m in range(2):
            total = product(t, m, ours)
            if m == 0:
                links.recv(cores + t, fpair.at[t], sib)
            fsum[t, m] = (total + fpair[t, m].astype(jnp.float32)).astype(BF)
            for e in range(2):
                away, cp = outgoing(t, m, e)

                @pl.when(away)
                def _():
                    cp.start()

                @pl.when(jnp.logical_not(away))
                def _():
                    got[column_slice((y + 4 - t) % 4, z), x] = fsum[t, m, e * 128:(e + 1) * 128]

    turns = (0, 1, 3, 2)
    start_slice(turns[0])
    for before, t in zip(turns, turns[1:]):
        finish_slice(before)
        start_slice(t)
    finish_slice(turns[-1])
    for j in range(4):
        sig[:, j * 128:(j + 1) * 128] = rows[j, y].reshape(256, 128)

    for t in turns:
        slot = column_slice((from_y + 4 - t) % 4, z)
        for q in range(4):
            frm = from_y * 8 + q * 2 + c

            @pl.when(frm != r)
            def _():
                links.recv(over_x + 4 * t + q, got.at[slot, q], (frm, z))
    for j in range(4):
        total = got[j, 0].astype(jnp.float32)
        for q in range(1, 4):
            total = total + got[j, q].astype(jnp.float32)
        front[:, j * 128:(j + 1) * 128] = total
    for t in turns:
        for m in range(2):
            for e in range(2):
                away, cp = outgoing(t, m, e)

                @pl.when(away)
                def _():
                    cp.wait_send()
    links.drain()


def per_device(sigma_anc, lower_off, inverse_diag, structure):
    nsem = 272
    negated, front = pl.pallas_call(
        mega,
        out_shape=(jax.ShapeDtypeStruct((256, 512), BF), jax.ShapeDtypeStruct((128, 512), jnp.float32)),
        in_specs=[ANY, ANY, VM, SM], out_specs=[VM, VM],
        scratch_shapes=[
            pltpu.SemaphoreType.DMA((nsem,)), pltpu.SemaphoreType.DMA((nsem,)), pltpu.SemaphoreType.DMA((4,)),
            pltpu.VMEM((40, 5, 8, 256), jnp.float32), pltpu.VMEM((8, 160, 256), BF),
            pltpu.VMEM((8, 256, 512), BF), pltpu.VMEM((4, 4, 2, 128, 512), BF), pltpu.VMEM((512, 128), BF),
            pltpu.VMEM((8, 160, 256), BF), pltpu.VMEM((320, 1024), BF), pltpu.VMEM((4, 320, 1024), BF),
            pltpu.VMEM((256, 512), jnp.float32), pltpu.VMEM((4, 256, 128), BF), pltpu.VMEM((8, 1024, 128), BF),
            pltpu.VMEM((8, 512, 128), BF),
            pltpu.VMEM((5, 4, 2, 160, 256), BF), pltpu.VMEM((5, 4, 160, 256), BF),
            pltpu.VMEM((5, 4, 160, 256), BF), pltpu.VMEM((5, 3, 160, 256), BF),
            pltpu.VMEM((8, 5, 32, 128), BF), pltpu.VMEM((40, 32, 128), BF), pltpu.VMEM((8, 4, 32, 128), BF),
            pltpu.VMEM((4, 4, 8, 32, 128), BF), pltpu.VMEM((4, 2, 256, 128), BF), pltpu.VMEM((4, 2, 256, 128), BF),
            pltpu.VMEM((4, 2, 256, 128), BF), pltpu.VMEM((4, 4, 128, 128), BF),
            pltpu.VMEM((4, 4, 256, 128), jnp.float32), pltpu.VMEM((4, 256, 1024), BF)],
        compiler_params=pltpu.CompilerParams(
            collective_id=1, has_side_effects=True, vmem_limit_bytes=60 * 2**20),
        name="selected_inverse")(lower_off, inverse_diag, sigma_anc, structure)
    return pl.pallas_call(
        finish,
        out_shape=(jax.ShapeDtypeStruct((256, 512), BF), jax.ShapeDtypeStruct((128, 512), jnp.float32)),
        in_specs=[VM, VM], out_specs=[VM, VM], name="finish")(negated, front)


def solution(mesh):
    in_specs = (P("col", "row", None), P("row", "col"), P("row", "col"), P())
    out_specs = (P("row", "col"), P("row", "col"))
    return jax.shard_map(
        per_device, mesh=mesh, in_specs=in_specs, out_specs=out_specs, check_vma=False
    )
```

```python
import functools

import jax
import jax.numpy as jnp
from jax import lax
from jax.experimental import pallas as pl
from jax.experimental.pallas import tpu as pltpu
from jax.sharding import PartitionSpec as P

MESH = pl.DeviceIdType.MESH
NX, NY, NC, NZ = 4, 4, 2, 8
ANY = pl.BlockSpec(memory_space=pl.ANY)
VM = pl.BlockSpec(memory_space=pltpu.VMEM)
SM = pl.BlockSpec(memory_space=pltpu.SMEM)
BF = jnp.bfloat16


def coords():
    r = lax.axis_index("row")
    return r // 8, (r // 2) % 4, r % 2, lax.axis_index("col")


def column_slice(y, z):
    return (y + z // 2) % 4


def dev(y, x, c, z):
    return ((y * NX + x) * NC + c, z)


class Links:
    def __init__(self, ss, rs):
        self.ss, self.rs, self.at, self.out = ss, rs, 0, []

    def slot(self, count=1):
        first = self.at
        self.at += count
        return first

    def send(self, i, src, dst, to):
        cp = pltpu.make_async_remote_copy(
            src_ref=src, dst_ref=dst, send_sem=self.ss.at[i], recv_sem=self.rs.at[i],
            device_id=to, device_id_type=MESH)
        cp.start()
        self.out.append(cp)

    def recv(self, i, dst, frm):
        pltpu.make_async_remote_copy(
            src_ref=dst, dst_ref=dst, send_sem=self.ss.at[i], recv_sem=self.rs.at[i],
            device_id=frm, device_id_type=MESH).wait_recv()

    def drain(self):
        for cp in self.out:
            cp.wait_send()


def ring(links, n, me, nxt, prv, view, own=None, pieces=2, pause=False):
    steps, half = n // 2, pieces // 2
    base = links.slot(2 * pieces * steps)
    own = own or (lambda h: view(me, h))
    idx = lambda d, s, h: base + (d * steps + s) * pieces + h
    for s in range(steps):
        for pos in range(half if s == steps - 1 else pieces):
            if pause and s == 0 and pos == half:
                yield
            for d, h in ((0, pos), (1, pieces - 1 - pos)):
                shard = lax.rem(me + (n - s if d == 0 else s), n)
                if s:
                    yield
                    links.recv(idx(d, s - 1, h), view(shard, h), prv if d == 0 else nxt)
                src = own(h) if s == 0 else view(shard, h)
                links.send(idx(d, s, h), src, view(shard, h), nxt if d == 0 else prv)
    for s, first in ((steps - 2, half), (steps - 1, 0)):
        yield
        for pos in range(first, first + half):
            for d, h in ((0, pos), (1, pieces - 1 - pos)):
                shard = lax.rem(me + (n - s - 1 if d == 0 else s + 1), n)
                links.recv(idx(d, s, h), view(shard, h), prv if d == 0 else nxt)


def pull(gen):
    try:
        next(gen)
        return True
    except StopIteration:
        return False


def pulls(gen, count):
    for _ in range(count):
        pull(gen)


def run(*gens):
    live = list(gens)
    while live:
        for g in list(live):
            try:
                next(g)
            except StopIteration:
                live.remove(g)


def finish(negated, total, sig, front):
    sig[...] = -negated[...]
    front[...] = total[...]


def mega(low, diag, anc, structure, sig, front, ss, rs, ls, ancb, ssel,

         strip, dcols, dshard, s1, sblk, sfull, acc, ush, ubuf, dbuf,
         part, pbuf, abuf, xbuf, fin, zbuf, snd, rows, fp, fpair, fsum, got, fpd, utr):
    y, x, c, z = coords()
    g = x * 2 + c
    r = y * 8 + g
    links = Links(ss, rs)
    zdev = [dev(y, x, c, (z + d) % NZ) for d in range(8)]
    xdev = [dev(y, (x + d) % NX, c, z) for d in range(4)]
    ydev = [dev((y + d) % NY, x, c, z) for d in range(4)]
    ysrc = [(y + 4 - d) % NY for d in range(4)]
    sib = dev(y, x, 1 - c, z)
    plane = [(t, q) for t in range(4) for q in range(8)][1:]
    peer = lambda t, q: (((y + t) % NY) * 8 + (g + q) % 8, z)
    near_by = [zdev[1], zdev[7]] + [peer(0, q) for q in range(1, 8)] + ydev[1:]
    entry = pltpu.get_barrier_semaphore()
    for other in near_by:
        pl.semaphore_signal(entry, inc=1, device_id=other, device_id_type=MESH)
    for k in range(40):
        ancb[k] = anc[:, :, k * 256:(k + 1) * 256].astype(jnp.float32)
    for q in range(8):
        picked = [ancb[structure[8 * t + q]].reshape(40, 256) for t in range(4)]
        ssel[q] = jnp.concatenate(picked, axis=0).astype(BF)
    pl.semaphore_wait(entry, len(near_by))

    a, b = pl.ds(0, 96), pl.ds(96, 32)
    dslot = lambda t: dshard.at[pl.ds(pl.multiple_of(t * 128, 128), 128)]
    dsl = lambda t: diag.at[:, pl.ds(pl.multiple_of(column_slice(t, z) * 128, 128), 128)]
    local = [
        pltpu.make_async_copy(low, strip.at[z], ls.at[0]),
        pltpu.make_async_copy(diag, dcols.at[y, x, c], ls.at[1]),
        pltpu.make_async_copy(ssel.at[g], s1.at[g], ls.at[2]),
        pltpu.make_async_copy(dsl(y), dslot(y), ls.at[3]),
    ]
    lgen = ring(links, NZ, z, zdev[1], zdev[7], lambda t, h: strip.at[t, pl.ds(h * 64, 64)],
                lambda h: low.at[pl.ds(h * 64, 64)], 4)
    pull(lgen)
    a1 = ring(links, NY, y, ydev[1], ydev[3], lambda t, h: dcols.at[t, x, c, pl.ds(h * 48, 48)],
              lambda h: diag.at[pl.ds(h * 48, 48)])
    b1 = ring(links, NX, x, xdev[1], xdev[3], lambda t, h: dcols.at[y, t, c, pl.ds(96 + h * 16, 16)],
              lambda h: diag.at[pl.ds(96 + h * 16, 16)])
    pull(a1)
    pull(b1)
    first = links.slot(10)
    for d in (3, 2, 4, 1, 5, 0, 6):
        q = (g + d + 1) % 8
        links.send(first + d, ssel.at[q], s1.at[g], dev(y, q // 2, q % 2, z))
    for cp in (local[1], local[0], local[2], local[3]):
        cp.start()
    run(a1, b1)
    local[1].wait()
    a2 = ring(links, NX, x, xdev[1], xdev[3], lambda t, h: dcols.at[pl.ds(2 * h, 2), t, c, a])
    b2 = ring(links, NY, y, ydev[1], ydev[3], lambda t, h: dcols.at[t, pl.ds(2 * h, 2), c, b])
    pull(a2)
    pull(b2)
    for d in range(3):
        links.send(first + 7 + d, dsl(y + d + 1), dslot(y), ydev[d + 1])
    sibs = links.slot(8)

    def share(k, d):
        t = (x + 4 - d) % NX
        links.send(sibs + k, dcols.at[:, t, c, a], dcols.at[:, t, c, a], sib)
        t = ysrc[d]
        links.send(sibs + k + 1, dcols.at[t, :, c, b], dcols.at[t, :, c, b], sib)

    share(0, 0)
    pulls(lgen, 8)

    local[2].wait()
    for d in range(7):
        s = (g + 8 - d - 1) % 8
        links.recv(first + d, s1.at[s], dev(y, s // 2, s % 2, z))

    @pl.loop(0, 2)
    def _(h):
        parts = [s1[4 * h + q].astype(jnp.float32).reshape(4, 5, 8, 256) for q in range(4)]
        for kb in range(4):
            for blk in range(5):
                tile = jnp.concatenate([p[kb, blk] for p in parts], axis=0).astype(BF)
                at = pl.ds(pl.multiple_of(h * 160 + blk * 32, 32), 32)
                sblk[at, kb * 256:(kb + 1) * 256] = tile

    keep = pltpu.make_async_copy(sblk, sfull.at[y], ls.at[2])
    keep.start()
    sgen = ring(links, NY, y, ydev[1], ydev[3], lambda t, h: sfull.at[t, pl.ds(h * 160, 160)],
                lambda h: sblk.at[pl.ds(h * 160, 160)], pause=True)
    pull(sgen)
    for _ in range(2):
        pulls(lgen, 4)
        pull(a2)
        pull(b2)
    pull(a2)
    pull(b2)
    share(2, 1)
    share(4, 3)
    pull(sgen)
    pulls(lgen, 4)
    pull(a2)
    pull(b2)
    share(6, 2)
    local[3].wait()
    for d in range(3):
        links.recv(first + 7 + d, dslot(ysrc[d + 1]), ydev[3 - d])
    dgen = ring(links, NZ, z, zdev[1], zdev[7], lambda t, h: dbuf.at[t, pl.ds(h * 256, 256)],
                lambda h: dshard.at[pl.ds(h * 256, 256)])
    dkeep = pltpu.make_async_copy(dshard, dbuf.at[z], ls.at[3])
    dkeep.start()
    pull(dgen)
    while pull(lgen):
        pass
    for k, d in ((0, 0), (2, 1), (4, 3), (6, 2)):
        t = (x + 4 - d) % NX
        links.recv(sibs + k, dcols.at[:, t, 1 - c, a], sib)
        t = ysrc[d]
        links.recv(sibs + k + 1, dcols.at[t, :, 1 - c, b], sib)
    local[0].wait()

    acc[...] = jnp.zeros_like(acc)

    @pl.loop(0, 8)
    def _(k):
        right = dcols[k // 2, pl.ds((k % 2) * 2, 2)].reshape(512, 512)
        acc[...] += jnp.dot(strip[k], right, preferred_element_type=jnp.float32)

    for j in range(4):
        ush[j] = acc[:, j * 128:(j + 1) * 128].astype(BF)

    kblock = lambda t: pl.ds(pl.multiple_of(t * 256, 256), 256)
    own = pltpu.make_async_copy(ush.at[column_slice(y, z)], ubuf.at[z, kblock(y)], ls.at[0])
    base = links.slot(3)
    for d in range(3):
        links.send(base + d, ush.at[column_slice(y + d + 1, z)], ubuf.at[z, kblock(y)], ydev[d + 1])
    own.start()
    own.wait()
    for d in range(3):
        links.recv(base + d, ubuf.at[z, kblock(ysrc[d + 1])], ydev[3 - d])
    ugen = ring(links, NZ, z, zdev[1], zdev[7], lambda t, h: ubuf.at[t, pl.ds(h * 256, 256)], pieces=4)
    pull(ugen)
    pulls(sgen, 2)

    pair, xs, zs = links.slot(5), links.slot(15), links.slot(8)
    slab = lambda k: zbuf.at[pl.ds(k * 5, 5)]
    zkeep = pltpu.make_async_copy(fin.at[z], slab(z), ls.at[1])

    def shards(k):
        return ((z,), *[((z + d) % NZ, (z + NZ - d) % NZ) for d in (1, 2, 3)], ((z + 4) % NZ,))[k]

    def multiply(k):
        ids = shards(k)
        n = 128 * len(ids)
        right = jnp.concatenate([ubuf[t] for t in ids], axis=1) if len(ids) == 2 else ubuf[ids[0]]

        @pl.loop(0, 4)
        def _(i):
            total = jnp.dot(sfull[i], right, preferred_element_type=jnp.float32).astype(BF)
            part[k, i, 0, :, :n] = total[:160]
            part[k, i, 1, :, :n] = total[160:]

        links.send(pair + k, part.at[k, :, 1 - c, :, pl.ds(0, n)], pbuf.at[k, :, :, pl.ds(0, n)], sib)

    def across(k):
        n = 128 * len(shards(k))
        links.recv(pair + k, pbuf.at[k, :, :, pl.ds(0, n)], sib)

        @pl.loop(0, 4)
        def _(i):
            @pl.loop(0, 5)
            def _(j):
                at = pl.ds(pl.multiple_of(j * 32, 32), 32)
                total = part[k, i, c, at, :n].astype(jnp.float32) + pbuf[k, i, at, :n].astype(jnp.float32)
                abuf[k, i, at, :n] = total.astype(BF)

        for d in (2, 1, 3):
            links.send(xs + 3 * k + d - 1, abuf.at[k, (x + d) % NX, :, pl.ds(0, n)],
                       xbuf.at[k, d - 1, :, pl.ds(0, n)], xdev[d])

    def onward(k):
        ids = shards(k)
        n = 128 * len(ids)
        for d in (1, 3, 2):
            links.recv(xs + 3 * k + d - 1, xbuf.at[k, d - 1, :, pl.ds(0, n)], xdev[4 - d])

        @pl.loop(0, 5)
        def _(j):
            at = pl.ds(pl.multiple_of(j * 32, 32), 32)
            total = abuf[k, x, at, :n].astype(jnp.float32)
            for d in range(3):
                total = total + xbuf[k, d, at, :n].astype(jnp.float32)
            total = total.astype(BF)
            for m, t in enumerate(ids):
                fin[t, j] = total[:, m * 128:(m + 1) * 128]

        if k == 0:
            zkeep.start()
        else:
            for d in sorted({k, NZ - k}):
                links.send(zs + d, fin.at[(z + d) % NZ], slab(z), zdev[d])

    pulls(ugen, 8)
    while pull(sgen):
        pass
    keep.wait()
    multiply(0)
    pulls(ugen, 4)
    multiply(1)
    across(0)
    pulls(ugen, 4)
    multiply(2)
    across(1)
    onward(0)
    pulls(ugen, 5)
    multiply(3)
    across(2)
    onward(1)
    pull(ugen)
    multiply(4)
    across(3)
    onward(2)
    across(4)
    onward(3)
    onward(4)
    for k in range(8):
        utr[k // 2, (k % 2) * 128:(k % 2 + 1) * 128] = jnp.transpose(ubuf[k])
    pulls(dgen, 4)
    zkeep.wait()
    for d in (1, 7, 2, 6, 3, 5, 4):
        links.recv(zs + d, slab((z + 8 - d) % NZ), zdev[8 - d])

    ps = links.slot(32)
    for q in range(8):
        for t in range(4):
            snd[q, t] = zbuf[structure[8 * t + q]]
    spot = lambda yy, gg: rows.at[column_slice(yy, z), :, gg]
    for t in (0, 1, 3, 2):
        for q in range(1 if t == 0 else 0, 8):
            links.send(ps + 8 * t + q, snd.at[(g + q) % 8], spot(y, g), peer(t, q))
    home = pltpu.make_async_copy(snd.at[g], spot(y, g), ls.at[0])
    home.start()
    while pull(dgen):
        pass
    dkeep.wait()
    over_rows = (((0,), (0,)), ((), ()))
    drows = dcols[:, x, c].reshape(512, 512)
    for k in range(8):
        at = pl.ds((k % 2) * 128, 128)
        both = lax.dot_general(dbuf[k], drows, over_rows, preferred_element_type=jnp.float32)
        for j in range(4):
            fpd[j, k // 2, at] = both[:, j * 128:(j + 1) * 128]
    home.wait()

    cores, over_x = links.slot(4), links.slot(16)
    from_y = (r % 4 + 4 - y) % 4
    theirs, ours = (y + 1 - c) % 2, (y + c) % 2

    def product(t, m, kind):
        k = 2 * m + kind
        slot = column_slice((y + 4 - t) % 4, z)
        right = rows[slot].reshape(1024, 128)
        return fpd[slot, k] + jnp.dot(utr[k], right, preferred_element_type=jnp.float32)

    def start_slice(t):
        for q in range(1 if t == 0 else 0, 8):
            links.recv(ps + 8 * t + q, spot((y + 4 - t) % 4, (g + 8 - q) % 8), peer(4 - t, 8 - q))
        for m in range(2):
            fp[t, m] = product(t, m, theirs).astype(BF)
        links.send(cores + t, fp.at[t], fpair.at[t], sib)

    def outgoing(t, m, e):
        k = 2 * m + ours
        to = (k * 8 + (2 * e + (y + k) % 4 // 2) * 2 + c, z)
        i = over_x + 4 * t
        return to[0] != r, pltpu.make_async_remote_copy(
            src_ref=fsum.at[t, m, pl.ds(e * 128, 128)], dst_ref=got.at[column_slice((y + 4 - t) % 4, z), x],
            send_sem=ss.at[i + 2 * m + e], recv_sem=rs.at[i + x], device_id=to, device_id_type=MESH)

    def finish_slice(t):
        for m in range(2):
            total = product(t, m, ours)
            if m == 0:
                links.recv(cores + t, fpair.at[t], sib)
            fsum[t, m] = (total + fpair[t, m].astype(jnp.float32)).astype(BF)
            for e in range(2):
                away, cp = outgoing(t, m, e)

                @pl.when(away)
                def _():
                    cp.start()

                @pl.when(jnp.logical_not(away))
                def _():
                    got[column_slice((y + 4 - t) % 4, z), x] = fsum[t, m, e * 128:(e + 1) * 128]

    turns = (0, 1, 3, 2)
    start_slice(turns[0])
    for before, t in zip(turns, turns[1:]):
        finish_slice(before)
        start_slice(t)
    finish_slice(turns[-1])
    for j in range(4):
        sig[:, j * 128:(j + 1) * 128] = rows[j, y].reshape(256, 128)

    for t in turns:
        slot = column_slice((from_y + 4 - t) % 4, z)
        for q in range(4):
            frm = from_y * 8 + q * 2 + c

            @pl.when(frm != r)
            def _():
                links.recv(over_x + 4 * t + q, got.at[slot, q], (frm, z))
    for j in range(4):
        total = got[j, 0].astype(jnp.float32)
        for q in range(1, 4):
            total = total + got[j, q].astype(jnp.float32)
        front[:, j * 128:(j + 1) * 128] = total
    for t in turns:
        for m in range(2):
            for e in range(2):
                away, cp = outgoing(t, m, e)

                @pl.when(away)
                def _():
                    cp.wait_send()
    links.drain()


def per_device(sigma_anc, lower_off, inverse_diag, structure):
    nsem = 272
    negated, front = pl.pallas_call(
        mega,
        out_shape=(jax.ShapeDtypeStruct((256, 512), BF), jax.ShapeDtypeStruct((128, 512), jnp.float32)),
        in_specs=[ANY, ANY, VM, SM], out_specs=[VM, VM],
        scratch_shapes=[
            pltpu.SemaphoreType.DMA((nsem,)), pltpu.SemaphoreType.DMA((nsem,)), pltpu.SemaphoreType.DMA((4,)),
            pltpu.VMEM((40, 5, 8, 256), jnp.float32), pltpu.VMEM((8, 160, 256), BF),
            pltpu.VMEM((8, 256, 512), BF), pltpu.VMEM((4, 4, 2, 128, 512), BF), pltpu.VMEM((512, 128), BF),
            pltpu.VMEM((8, 160, 256), BF), pltpu.VMEM((320, 1024), BF), pltpu.VMEM((4, 320, 1024), BF),
            pltpu.VMEM((256, 512), jnp.float32), pltpu.VMEM((4, 256, 128), BF), pltpu.VMEM((8, 1024, 128), BF),
            pltpu.VMEM((8, 512, 128), BF),
            pltpu.VMEM((5, 4, 2, 160, 256), BF), pltpu.VMEM((5, 4, 160, 256), BF),
            pltpu.VMEM((5, 4, 160, 256), BF), pltpu.VMEM((5, 3, 160, 256), BF),
            pltpu.VMEM((8, 5, 32, 128), BF), pltpu.VMEM((40, 32, 128), BF), pltpu.VMEM((8, 4, 32, 128), BF),
            pltpu.VMEM((4, 4, 8, 32, 128), BF), pltpu.VMEM((4, 2, 256, 128), BF), pltpu.VMEM((4, 2, 256, 128), BF),
            pltpu.VMEM((4, 2, 256, 128), BF), pltpu.VMEM((4, 4, 128, 128), BF),
            pltpu.VMEM((4, 4, 256, 128), jnp.float32), pltpu.VMEM((4, 256, 1024), BF)],
        compiler_params=pltpu.CompilerParams(
            collective_id=1, has_side_effects=True, vmem_limit_bytes=60 * 2**20),
        name="selected_inverse")(lower_off, inverse_diag, sigma_anc, structure)
    return pl.pallas_call(
        finish,
        out_shape=(jax.ShapeDtypeStruct((256, 512), BF), jax.ShapeDtypeStruct((128, 512), jnp.float32)),
        in_specs=[VM, VM], out_specs=[VM, VM], name="finish")(negated, front)


def solution(mesh):
    in_specs = (P("col", "row", None), P("row", "col"), P("row", "col"), P())
    out_specs = (P("row", "col"), P("row", "col"))
    return jax.shard_map(
        per_device, mesh=mesh, in_specs=in_specs, out_specs=out_specs, check_vma=False
    )
```

```python
import functools

import jax
import jax.numpy as jnp
from jax import lax
from jax.experimental import pallas as pl
from jax.experimental.pallas import tpu as pltpu
from jax.sharding import PartitionSpec as P

MESH = pl.DeviceIdType.MESH
NX, NY, NC, NZ = 4, 4, 2, 8
ANY = pl.BlockSpec(memory_space=pl.ANY)
VM = pl.BlockSpec(memory_space=pltpu.VMEM)
SM = pl.BlockSpec(memory_space=pltpu.SMEM)
BF = jnp.bfloat16


def coords():
    r = lax.axis_index("row")
    return r // 8, (r // 2) % 4, r % 2, lax.axis_index("col")


def column_slice(y, z):
    return (y + z // 2) % 4


def dev(y, x, c, z):
    return ((y * NX + x) * NC + c, z)


class Links:
    def __init__(self, ss, rs):
        self.ss, self.rs, self.at, self.out = ss, rs, 0, []

    def slot(self, count=1):
        first = self.at
        self.at += count
        return first

    def send(self, i, src, dst, to):
        cp = pltpu.make_async_remote_copy(
            src_ref=src, dst_ref=dst, send_sem=self.ss.at[i], recv_sem=self.rs.at[i],
            device_id=to, device_id_type=MESH)
        cp.start()
        self.out.append(cp)

    def recv(self, i, dst, frm):
        pltpu.make_async_remote_copy(
            src_ref=dst, dst_ref=dst, send_sem=self.ss.at[i], recv_sem=self.rs.at[i],
            device_id=frm, device_id_type=MESH).wait_recv()

    def drain(self):
        for cp in self.out:
            cp.wait_send()


def ring(links, n, me, nxt, prv, view, own=None, pieces=2, pause=False):
    steps, half = n // 2, pieces // 2
    base = links.slot(2 * pieces * steps)
    own = own or (lambda h: view(me, h))
    idx = lambda d, s, h: base + (d * steps + s) * pieces + h
    for s in range(steps):
        for pos in range(half if s == steps - 1 else pieces):
            if pause and s == 0 and pos == half:
                yield
            for d, h in ((0, pos), (1, pieces - 1 - pos)):
                shard = lax.rem(me + (n - s if d == 0 else s), n)
                if s:
                    yield
                    links.recv(idx(d, s - 1, h), view(shard, h), prv if d == 0 else nxt)
                src = own(h) if s == 0 else view(shard, h)
                links.send(idx(d, s, h), src, view(shard, h), nxt if d == 0 else prv)
    for s, first in ((steps - 2, half), (steps - 1, 0)):
        yield
        for pos in range(first, first + half):
            for d, h in ((0, pos), (1, pieces - 1 - pos)):
                shard = lax.rem(me + (n - s - 1 if d == 0 else s + 1), n)
                links.recv(idx(d, s, h), view(shard, h), prv if d == 0 else nxt)


def pull(gen):
    try:
        next(gen)
        return True
    except StopIteration:
        return False


def pulls(gen, count):
    for _ in range(count):
        pull(gen)


def run(*gens):
    live = list(gens)
    while live:
        for g in list(live):
            try:
                next(g)
            except StopIteration:
                live.remove(g)


def finish(negated, total, sig, front):
    sig[...] = -negated[...]
    front[...] = total[...]


def mega(low, diag, anc, structure, sig, front, ss, rs, ls, ancb, ssel,

         strip, dcols, dshard, s1, sblk, sfull, acc, ush, ubuf, dbuf,
         part, pbuf, abuf, xbuf, fin, zbuf, snd, rows, fp, fpair, fsum, got, fpd, utr):
    y, x, c, z = coords()
    g = x * 2 + c
    r = y * 8 + g
    links = Links(ss, rs)
    zdev = [dev(y, x, c, (z + d) % NZ) for d in range(8)]
    xdev = [dev(y, (x + d) % NX, c, z) for d in range(4)]
    ydev = [dev((y + d) % NY, x, c, z) for d in range(4)]
    ysrc = [(y + 4 - d) % NY for d in range(4)]
    sib = dev(y, x, 1 - c, z)
    plane = [(t, q) for t in range(4) for q in range(8)][1:]
    peer = lambda t, q: (((y + t) % NY) * 8 + (g + q) % 8, z)
    near_by = [zdev[1], zdev[7]] + [peer(0, q) for q in range(1, 8)] + ydev[1:]
    entry = pltpu.get_barrier_semaphore()
    for other in near_by:
        pl.semaphore_signal(entry, inc=1, device_id=other, device_id_type=MESH)
    dslot = lambda t: dshard.at[pl.ds(pl.multiple_of(t * 128, 128), 128)]
    dsl = lambda t: diag.at[:, pl.ds(pl.multiple_of(column_slice(t, z) * 128, 128), 128)]
    local = [
        pltpu.make_async_copy(low, strip.at[z], ls.at[0]),
        pltpu.make_async_copy(diag, dcols.at[y, x, c], ls.at[1]),
        pltpu.make_async_copy(ssel.at[g], s1.at[g], ls.at[2]),
        pltpu.make_async_copy(dsl(y), dslot(y), ls.at[3]),
    ]
    for k in (0, 1, 3):
        local[k].start()
    for k in range(40):
        ancb[k] = anc[:, :, k * 256:(k + 1) * 256].astype(jnp.float32)
    for q in range(8):
        picked = [ancb[structure[8 * t + q]].reshape(40, 256) for t in range(4)]
        ssel[q] = jnp.concatenate(picked, axis=0).astype(BF)
    local[2].start()
    pl.semaphore_wait(entry, len(near_by))
    local[0].wait()
    local[1].wait()

    a, b = pl.ds(0, 96), pl.ds(96, 32)
    lgen = ring(links, NZ, z, zdev[1], zdev[7], lambda t, h: strip.at[t, pl.ds(h * 64, 64)],
                pieces=4)
    pull(lgen)
    a1 = ring(links, NY, y, ydev[1], ydev[3], lambda t, h: dcols.at[t, x, c, pl.ds(h * 48, 48)])
    b1 = ring(links, NX, x, xdev[1], xdev[3], lambda t, h: dcols.at[y, t, c, pl.ds(96 + h * 16, 16)])
    pull(a1)
    pull(b1)
    first = links.slot(10)
    for d in (3, 2, 4, 1, 5, 0, 6):
        q = (g + d + 1) % 8
        links.send(first + d, ssel.at[q], s1.at[g], dev(y, q // 2, q % 2, z))
    run(a1, b1)
    a2 = ring(links, NX, x, xdev[1], xdev[3], lambda t, h: dcols.at[pl.ds(2 * h, 2), t, c, a])
    b2 = ring(links, NY, y, ydev[1], ydev[3], lambda t, h: dcols.at[t, pl.ds(2 * h, 2), c, b])
    pull(a2)
    pull(b2)
    for d in range(3):
        links.send(first + 7 + d, dsl(y + d + 1), dslot(y), ydev[d + 1])
    sibs = links.slot(8)

    def share(k, d):
        t = (x + 4 - d) % NX
        links.send(sibs + k, dcols.at[:, t, c, a], dcols.at[:, t, c, a], sib)
        t = ysrc[d]
        links.send(sibs + k + 1, dcols.at[t, :, c, b], dcols.at[t, :, c, b], sib)

    share(0, 0)
    pulls(lgen, 8)

    local[2].wait()
    for d in range(7):
        s = (g + 8 - d - 1) % 8
        links.recv(first + d, s1.at[s], dev(y, s // 2, s % 2, z))

    @pl.loop(0, 2)
    def _(h):
        parts = [s1[4 * h + q].astype(jnp.float32).reshape(4, 5, 8, 256) for q in range(4)]
        for kb in range(4):
            for blk in range(5):
                tile = jnp.concatenate([p[kb, blk] for p in parts], axis=0).astype(BF)
                at = pl.ds(pl.multiple_of(h * 160 + blk * 32, 32), 32)
                sblk[at, kb * 256:(kb + 1) * 256] = tile

    keep = pltpu.make_async_copy(sblk, sfull.at[y], ls.at[2])
    keep.start()
    sgen = ring(links, NY, y, ydev[1], ydev[3], lambda t, h: sfull.at[t, pl.ds(h * 160, 160)],
                lambda h: sblk.at[pl.ds(h * 160, 160)], pause=True)
    pull(sgen)
    for _ in range(2):
        pulls(lgen, 4)
        pull(a2)
        pull(b2)
    pull(a2)
    pull(b2)
    share(2, 1)
    share(4, 3)
    pull(sgen)
    pulls(lgen, 4)
    pull(a2)
    pull(b2)
    share(6, 2)
    local[3].wait()
    for d in range(3):
        links.recv(first + 7 + d, dslot(ysrc[d + 1]), ydev[3 - d])
    dgen = ring(links, NZ, z, zdev[1], zdev[7], lambda t, h: dbuf.at[t, pl.ds(h * 256, 256)],
                lambda h: dshard.at[pl.ds(h * 256, 256)])
    dkeep = pltpu.make_async_copy(dshard, dbuf.at[z], ls.at[3])
    dkeep.start()
    pull(dgen)
    while pull(lgen):
        pass
    for k, d in ((0, 0), (2, 1), (4, 3), (6, 2)):
        t = (x + 4 - d) % NX
        links.recv(sibs + k, dcols.at[:, t, 1 - c, a], sib)
        t = ysrc[d]
        links.recv(sibs + k + 1, dcols.at[t, :, 1 - c, b], sib)

    acc[...] = jnp.zeros_like(acc)

    @pl.loop(0, 8)
    def _(k):
        right = dcols[k // 2, pl.ds((k % 2) * 2, 2)].reshape(512, 512)
        acc[...] += jnp.dot(strip[k], right, preferred_element_type=jnp.float32)

    for j in range(4):
        ush[j] = acc[:, j * 128:(j + 1) * 128].astype(BF)

    kblock = lambda t: pl.ds(pl.multiple_of(t * 256, 256), 256)
    own = pltpu.make_async_copy(ush.at[column_slice(y, z)], ubuf.at[z, kblock(y)], ls.at[0])
    base = links.slot(3)
    for d in range(3):
        links.send(base + d, ush.at[column_slice(y + d + 1, z)], ubuf.at[z, kblock(y)], ydev[d + 1])
    own.start()
    own.wait()
    for d in range(3):
        links.recv(base + d, ubuf.at[z, kblock(ysrc[d + 1])], ydev[3 - d])
    ugen = ring(links, NZ, z, zdev[1], zdev[7], lambda t, h: ubuf.at[t, pl.ds(h * 256, 256)], pieces=4)
    pull(ugen)
    pulls(sgen, 2)

    pair, xs, zs = links.slot(5), links.slot(15), links.slot(8)
    slab = lambda k: zbuf.at[pl.ds(k * 5, 5)]
    zkeep = pltpu.make_async_copy(fin.at[z], slab(z), ls.at[1])

    def shards(k):
        return ((z,), *[((z + d) % NZ, (z + NZ - d) % NZ) for d in (1, 2, 3)], ((z + 4) % NZ,))[k]

    def multiply(k):
        ids = shards(k)
        n = 128 * len(ids)
        right = jnp.concatenate([ubuf[t] for t in ids], axis=1) if len(ids) == 2 else ubuf[ids[0]]

        @pl.loop(0, 4)
        def _(i):
            total = jnp.dot(sfull[i], right, preferred_element_type=jnp.float32).astype(BF)
            part[k, i, 0, :, :n] = total[:160]
            part[k, i, 1, :, :n] = total[160:]

        links.send(pair + k, part.at[k, :, 1 - c, :, pl.ds(0, n)], pbuf.at[k, :, :, pl.ds(0, n)], sib)

    def across(k):
        n = 128 * len(shards(k))
        links.recv(pair + k, pbuf.at[k, :, :, pl.ds(0, n)], sib)

        @pl.loop(0, 4)
        def _(i):
            @pl.loop(0, 5)
            def _(j):
                at = pl.ds(pl.multiple_of(j * 32, 32), 32)
                total = part[k, i, c, at, :n].astype(jnp.float32) + pbuf[k, i, at, :n].astype(jnp.float32)
                abuf[k, i, at, :n] = total.astype(BF)

        for d in (2, 1, 3):
            links.send(xs + 3 * k + d - 1, abuf.at[k, (x + d) % NX, :, pl.ds(0, n)],
                       xbuf.at[k, d - 1, :, pl.ds(0, n)], xdev[d])

    def onward(k):
        ids = shards(k)
        n = 128 * len(ids)
        for d in (1, 3, 2):
            links.recv(xs + 3 * k + d - 1, xbuf.at[k, d - 1, :, pl.ds(0, n)], xdev[4 - d])

        @pl.loop(0, 5)
        def _(j):
            at = pl.ds(pl.multiple_of(j * 32, 32), 32)
            total = abuf[k, x, at, :n].astype(jnp.float32)
            for d in range(3):
                total = total + xbuf[k, d, at, :n].astype(jnp.float32)
            total = total.astype(BF)
            for m, t in enumerate(ids):
                fin[t, j] = total[:, m * 128:(m + 1) * 128]

        if k == 0:
            zkeep.start()
        else:
            for d in sorted({k, NZ - k}):
                links.send(zs + d, fin.at[(z + d) % NZ], slab(z), zdev[d])

    pulls(ugen, 8)
    while pull(sgen):
        pass
    keep.wait()
    multiply(0)
    pulls(ugen, 4)
    multiply(1)
    across(0)
    pulls(ugen, 4)
    multiply(2)
    across(1)
    onward(0)
    pulls(ugen, 5)
    multiply(3)
    across(2)
    onward(1)
    pull(ugen)
    multiply(4)
    across(3)
    onward(2)
    across(4)
    onward(3)
    onward(4)
    for k in range(8):
        utr[k // 2, (k % 2) * 128:(k % 2 + 1) * 128] = jnp.transpose(ubuf[k])
    pulls(dgen, 4)
    zkeep.wait()
    for d in (1, 7, 2, 6, 3, 5, 4):
        links.recv(zs + d, slab((z + 8 - d) % NZ), zdev[8 - d])

    ps = links.slot(32)
    for q in range(8):
        for t in range(4):
            snd[q, t] = zbuf[structure[8 * t + q]]
    spot = lambda yy, gg: rows.at[column_slice(yy, z), :, gg]
    for t in (0, 1, 3, 2):
        for q in range(1 if t == 0 else 0, 8):
            links.send(ps + 8 * t + q, snd.at[(g + q) % 8], spot(y, g), peer(t, q))
    home = pltpu.make_async_copy(snd.at[g], spot(y, g), ls.at[0])
    home.start()
    while pull(dgen):
        pass
    dkeep.wait()
    over_rows = (((0,), (0,)), ((), ()))
    drows = dcols[:, x, c].reshape(512, 512)
    for k in range(8):
        at = pl.ds((k % 2) * 128, 128)
        both = lax.dot_general(dbuf[k], drows, over_rows, preferred_element_type=jnp.float32)
        for j in range(4):
            fpd[j, k // 2, at] = both[:, j * 128:(j + 1) * 128]
    home.wait()

    cores, over_x = links.slot(4), links.slot(16)
    from_y = (r % 4 + 4 - y) % 4
    theirs, ours = (y + 1 - c) % 2, (y + c) % 2

    def product(t, m, kind):
        k = 2 * m + kind
        slot = column_slice((y + 4 - t) % 4, z)
        right = rows[slot].reshape(1024, 128)
        return fpd[slot, k] + jnp.dot(utr[k], right, preferred_element_type=jnp.float32)

    def start_slice(t):
        for q in range(1 if t == 0 else 0, 8):
            links.recv(ps + 8 * t + q, spot((y + 4 - t) % 4, (g + 8 - q) % 8), peer(4 - t, 8 - q))
        for m in range(2):
            fp[t, m] = product(t, m, theirs).astype(BF)
        links.send(cores + t, fp.at[t], fpair.at[t], sib)

    def outgoing(t, m, e):
        k = 2 * m + ours
        to = (k * 8 + (2 * e + (y + k) % 4 // 2) * 2 + c, z)
        i = over_x + 4 * t
        return to[0] != r, pltpu.make_async_remote_copy(
            src_ref=fsum.at[t, m, pl.ds(e * 128, 128)], dst_ref=got.at[column_slice((y + 4 - t) % 4, z), x],
            send_sem=ss.at[i + 2 * m + e], recv_sem=rs.at[i + x], device_id=to, device_id_type=MESH)

    def finish_slice(t):
        for m in range(2):
            total = product(t, m, ours)
            if m == 0:
                links.recv(cores + t, fpair.at[t], sib)
            fsum[t, m] = (total + fpair[t, m].astype(jnp.float32)).astype(BF)
            for e in range(2):
                away, cp = outgoing(t, m, e)

                @pl.when(away)
                def _():
                    cp.start()

                @pl.when(jnp.logical_not(away))
                def _():
                    got[column_slice((y + 4 - t) % 4, z), x] = fsum[t, m, e * 128:(e + 1) * 128]

    turns = (0, 1, 3, 2)
    start_slice(turns[0])
    for before, t in zip(turns, turns[1:]):
        finish_slice(before)
        start_slice(t)
    finish_slice(turns[-1])
    for j in range(4):
        sig[:, j * 128:(j + 1) * 128] = rows[j, y].reshape(256, 128)

    for t in turns:
        slot = column_slice((from_y + 4 - t) % 4, z)
        for q in range(4):
            frm = from_y * 8 + q * 2 + c

            @pl.when(frm != r)
            def _():
                links.recv(over_x + 4 * t + q, got.at[slot, q], (frm, z))
    for j in range(4):
        total = got[j, 0].astype(jnp.float32)
        for q in range(1, 4):
            total = total + got[j, q].astype(jnp.float32)
        front[:, j * 128:(j + 1) * 128] = total
    for t in turns:
        for m in range(2):
            for e in range(2):
                away, cp = outgoing(t, m, e)

                @pl.when(away)
                def _():
                    cp.wait_send()
    links.drain()


def per_device(sigma_anc, lower_off, inverse_diag, structure):
    nsem = 272
    negated, front = pl.pallas_call(
        mega,
        out_shape=(jax.ShapeDtypeStruct((256, 512), BF), jax.ShapeDtypeStruct((128, 512), jnp.float32)),
        in_specs=[ANY, ANY, VM, SM], out_specs=[VM, VM],
        scratch_shapes=[
            pltpu.SemaphoreType.DMA((nsem,)), pltpu.SemaphoreType.DMA((nsem,)), pltpu.SemaphoreType.DMA((4,)),
            pltpu.VMEM((40, 5, 8, 256), jnp.float32), pltpu.VMEM((8, 160, 256), BF),
            pltpu.VMEM((8, 256, 512), BF), pltpu.VMEM((4, 4, 2, 128, 512), BF), pltpu.VMEM((512, 128), BF),
            pltpu.VMEM((8, 160, 256), BF), pltpu.VMEM((320, 1024), BF), pltpu.VMEM((4, 320, 1024), BF),
            pltpu.VMEM((256, 512), jnp.float32), pltpu.VMEM((4, 256, 128), BF), pltpu.VMEM((8, 1024, 128), BF),
            pltpu.VMEM((8, 512, 128), BF),
            pltpu.VMEM((5, 4, 2, 160, 256), BF), pltpu.VMEM((5, 4, 160, 256), BF),
            pltpu.VMEM((5, 4, 160, 256), BF), pltpu.VMEM((5, 3, 160, 256), BF),
            pltpu.VMEM((8, 5, 32, 128), BF), pltpu.VMEM((40, 32, 128), BF), pltpu.VMEM((8, 4, 32, 128), BF),
            pltpu.VMEM((4, 4, 8, 32, 128), BF), pltpu.VMEM((4, 2, 256, 128), BF), pltpu.VMEM((4, 2, 256, 128), BF),
            pltpu.VMEM((4, 2, 256, 128), BF), pltpu.VMEM((4, 4, 128, 128), BF),
            pltpu.VMEM((4, 4, 256, 128), jnp.float32), pltpu.VMEM((4, 256, 1024), BF)],
        compiler_params=pltpu.CompilerParams(
            collective_id=1, has_side_effects=True, vmem_limit_bytes=60 * 2**20),
        name="selected_inverse")(lower_off, inverse_diag, sigma_anc, structure)
    return pl.pallas_call(
        finish,
        out_shape=(jax.ShapeDtypeStruct((256, 512), BF), jax.ShapeDtypeStruct((128, 512), jnp.float32)),
        in_specs=[VM, VM], out_specs=[VM, VM], name="finish")(negated, front)


def solution(mesh):
    in_specs = (P("col", "row", None), P("row", "col"), P("row", "col"), P())
    out_specs = (P("row", "col"), P("row", "col"))
    return jax.shard_map(
        per_device, mesh=mesh, in_specs=in_specs, out_specs=out_specs, check_vma=False
    )
```
